256 devices in a mesh: dom: 128 (over x, y, z_hi, core), band: 2 (over z_lo).
Axes of the slice: x: 4, y: 4, z: 8 (z_hi: 4, z_lo: 2; z = z_hi * 2 + z_lo), core: 2. Of those that a mesh axis runs over, the one named last changes fastest.
Arguments:
- orbitals: float32 [128, 2, 12, 32, 1024], P('dom', 'band'), may hold values from -500 to 500
- potential: float32 [128, 12, 32, 32], P('dom'), may hold values from -40 to 0
Outputs:
- orbitals_out: float32 [128, 2, 12, 32, 1024], P('dom', 'band')
- projected: float32 [64, 64], replicated
The draws below stay inside these ranges and needn't reach their ends.
All inputs are finite; a program needn't handle non-finite values.
Results may differ from the reference program's by a relative error of at most 0.00016.
Values sent between devices are 32-bit elements; how exact they have to be, the bound alone decides.
A program may use at most 64 MiB of HBM per device.

```python
import math
import jax
import jax.numpy as jnp
from jax import lax

CX = 12
CY = 32
CZ = 32
OB = 32
PY = 4
PZ = 4
PX = 8
TILES = 128
BLOCKS = 2
ORBITALS = 64
NX = 96
NY = 128
NZ = 128


def draw_orbitals(key, part):
    key = jax.random.fold_in(key, 11)
    base_key, orbital_key, tile_key = jax.random.split(key, 3)
    shape = (TILES, BLOCKS, CX, CY, CZ, OB)
    orbital_scale = jnp.exp(jax.random.uniform(orbital_key, (1, BLOCKS, 1, 1, 1, OB), jnp.float32) * math.log(10.0))
    tile_scale = jnp.exp(jax.random.uniform(tile_key, (TILES, 1, 1, 1, 1, 1), jnp.float32) * math.log(10.0))
    base = jnp.clip(jax.random.normal(base_key, shape, jnp.float32), -4.0, 4.0)
    return (base * orbital_scale * tile_scale).reshape(TILES, BLOCKS, CX, CY, CZ * OB).astype(jnp.float32)


def block_scale(key, extent, pieces, smallest, high):
    level, own = 1.0, jax.random.fold_in(key, 6)
    for position, shards_of in pieces:
        steps = jnp.exp(jax.random.uniform(jax.random.fold_in(own, position), (shards_of,), jnp.float32, smallest / len(pieces), high / len(pieces)))
        level = level * jnp.repeat(steps, extent[position] // shards_of).reshape([-1 if axis == position else 1 for axis in range(len(extent))])
    return level


def setup_inputs(seed: int = 0) -> dict:
    key_list = jax.random.split(jax.random.key(seed), 3)
    orbitals = draw_orbitals(jax.random.fold_in(key_list[2], 71), 0)
    potential = jnp.clip(-40.0 + 40.0 * jax.random.uniform(key_list[1], (TILES, CX, CY, CZ), jnp.float32) ** block_scale(key_list[1], (TILES, CX, CY, CZ), ((0, 128),), -0.2, 0.2), -40.0, 0.0)
    return dict(orbitals=orbitals, potential=potential)


COEFFS = (-5369.0 / 1800.0, 12.0 / 7.0, -15.0 / 56.0, 10.0 / 189.0, -1.0 / 112.0, 2.0 / 1925.0, -1.0 / 16632.0)
SPACING = 0.32
CENTER = 71.0
HALFWIDTH = 69.0

def scaled_operator(field, potential_grid):
    padded = jnp.pad(field, 6)
    nx, ny, nz = field.shape
    lap = 3.0 * COEFFS[0] * field
    for shift in range(1, 7):
        terms = padded[6 + shift:6 + shift + nx, 6:6 + ny, 6:6 + nz] + padded[6 - shift:6 - shift + nx, 6:6 + ny, 6:6 + nz]
        terms = terms + padded[6:6 + nx, 6 + shift:6 + shift + ny, 6:6 + nz] + padded[6:6 + nx, 6 - shift:6 - shift + ny, 6:6 + nz]
        terms = terms + padded[6:6 + nx, 6:6 + ny, 6 + shift:6 + shift + nz] + padded[6:6 + nx, 6:6 + ny, 6 - shift:6 - shift + nz]
        lap = lap + COEFFS[shift] * terms
    return (-0.5 / SPACING ** 2 * lap + potential_grid * field - CENTER * field) / HALFWIDTH

def reference(orbitals, potential):
    grid = orbitals.reshape(PX, PY, PZ, BLOCKS, CX, CY, CZ, OB).transpose(3, 7, 0, 4, 1, 5, 2, 6).reshape(ORBITALS, NX, NY, NZ)
    pot_grid = potential.reshape(PX, PY, PZ, CX, CY, CZ).transpose(0, 3, 1, 4, 2, 5).reshape(NX, NY, NZ)

    def filter_one(field):
        first = scaled_operator(field, pot_grid)
        filtered = 2.0 * scaled_operator(first, pot_grid) - field
        return (filtered, scaled_operator(filtered, pot_grid))
    filtered, image = lax.map(filter_one, grid)
    flat_f = filtered.reshape(ORBITALS, NX * NY * NZ)
    flat_w = image.reshape(ORBITALS, NX * NY * NZ)
    cells = NX * NY * NZ
    hi = lax.Precision.HIGHEST
    correlation = jnp.dot(flat_f, flat_f.T, precision=hi) / cells
    hamiltonian = jnp.dot(flat_f, flat_w.T, precision=hi) / cells
    lower = jnp.linalg.cholesky(correlation)
    inverse = jax.scipy.linalg.solve_triangular(lower, jnp.eye(ORBITALS, dtype=jnp.float32), lower=True)
    rotated = jnp.dot(inverse, flat_f, precision=hi)
    projected = jnp.dot(jnp.dot(inverse, hamiltonian, precision=hi), inverse.T, precision=hi)
    out = rotated.reshape(BLOCKS, OB, PX, CX, PY, CY, PZ, CZ).transpose(2, 4, 6, 0, 3, 5, 7, 1).reshape(TILES, BLOCKS, CX, CY, CZ * OB)
    return (out, projected)
```

```python
import functools

import jax
import jax.numpy as jnp
from jax import lax
from jax.experimental import pallas as pl
from jax.experimental.pallas import tpu as pltpu
from jax.sharding import PartitionSpec as P

COEFFS = (
    -5369.0 / 1800.0,
    12.0 / 7.0,
    -15.0 / 56.0,
    10.0 / 189.0,
    -1.0 / 112.0,
    2.0 / 1925.0,
    -1.0 / 16632.0,
)
SPACING = 0.32
CENTER = 71.0
HALFWIDTH = 69.0
KINETIC = -0.5 / SPACING**2 / HALFWIDTH
A = tuple(KINETIC * c for c in COEFFS)

CX, CY, CZ, OB = 12, 32, 32, 32
PX, PY, PZ = 8, 4, 4
NJ = CZ * OB // 128
CELLS = PX * CX * PY * CY * PZ * CZ
MESH = pl.DeviceIdType.MESH
HIGHEST = lax.Precision.HIGHEST
XO, JO, YO = 6, 2, 8
OWN = (pl.ds(XO, CX), pl.ds(JO, NJ), pl.ds(YO, CY))


def stencil(field, pot, x):
    lane = lax.broadcasted_iota(jnp.int32, (CY, 128), 1)

    def tile(j, dx=0, dy=0):
        return field[XO + x + dx, JO + j, pl.ds(YO + dy, CY), :]

    def partial(j):
        m2, m1, v, p1 = tile(j - 2), tile(j - 1), tile(j), tile(j + 1)
        t1 = A[3] * m1 + A[1] * v + A[5] * p1
        t2 = A[2] * (v + m1) + A[6] * (p1 + m2)
        t3 = A[3] * v + A[1] * m1 + A[5] * m2
        return (
            pltpu.roll(t1, 96, 1),
            pltpu.roll(t2, 64, 1),
            pltpu.roll(t3, 32, 1),
        )

    out = []
    low = partial(0)
    for j in range(NJ):
        high = partial(j + 1)
        acc = jnp.where(lane < 96, low[0], high[0])
        acc = acc + jnp.where(lane < 64, low[1], high[1])
        acc = acc + jnp.where(lane < 32, low[2], high[2])
        low = high
        acc = acc + pot[x, j] * tile(j)
        for k in range(1, 7):
            terms = tile(j, k) + tile(j, -k) + tile(j, 0, k) + tile(j, 0, -k)
            if k == 4:
                terms = terms + (tile(j + 1) + tile(j - 1))
            acc = acc + A[k] * terms
        out.append(acc)
    return out


def filter_kernel(
    orb_ref,
    pot_ref,
    filt_ref,
    band_ref,
    mats_ref,
    e0,
    e1,
    e2,
    img,
    pot,
    other,
    part,
    recv,
    load_sem,
    hs,
    hr,
    bs,
    br,
    rs,
    rr,
):
    dom = lax.axis_index("dom")
    band = lax.axis_index("band")
    tz = lax.rem(dom, PZ)
    ty = lax.rem(dom // PZ, PY)
    tx = dom // (PY * PZ)
    px, py, pz, core = dom // 32, lax.rem(dom // 8, 4), lax.rem(dom // 2, 4), lax.rem(dom, 2)

    loads = [
        pltpu.make_async_copy(
            orb_ref.at[0, 0, :, :, pl.ds(128 * j, 128)],
            e0.at[pl.ds(XO, CX), JO + j, pl.ds(YO, CY)],
            load_sem.at[j],
        )
        for j in range(NJ)
    ]
    for copy in loads:
        copy.start()

    def place(x, y, z, c):
        return ((x * 4 + y) * 4 + z) * 2 + c

    faces = (
        (PY * PZ, tx, PX),
        (PZ, ty, PY),
        (1, tz, PZ),
    )
    peers = [(place(px, py, pz, 1 - core), band), (dom, 1 - band)]
    zpeers = [(place(px, py, lax.rem(pz + k, 4), core), band) for k in range(1, 4)]
    ypeers = [(place(px, lax.rem(py + k, 4), pz, core), band) for k in range(1, 4)]
    xpeers = [(place(lax.rem(px + k, 4), py, pz, core), band) for k in range(1, 4)]

    barrier = pltpu.get_barrier_semaphore()
    count = jnp.int32(11)
    for peer in peers + zpeers + ypeers + xpeers:
        pl.semaphore_signal(barrier, inc=1, device_id=peer, device_id_type=MESH)
    for stride, at, n in faces:
        has_low, has_high = at > 0, at < n - 1
        count = count + has_low.astype(jnp.int32) + has_high.astype(jnp.int32)

        @pl.when(has_low)
        def _():
            pl.semaphore_signal(barrier, inc=1, device_id=(dom - stride, band), device_id_type=MESH)

        @pl.when(has_high)
        def _():
            pl.semaphore_signal(barrier, inc=1, device_id=(dom + stride, band), device_id_type=MESH)

    row = lax.broadcasted_iota(jnp.int32, (CZ, CZ * OB), 0)
    col = lax.broadcasted_iota(jnp.int32, (CZ, CZ * OB), 1)
    spread = (row == col // OB).astype(jnp.float32)

    def spread_pot(x, carry):
        scaled = (pot_ref[0, x] - CENTER) * (1.0 / HALFWIDTH) + 3.0 * A[0]
        wide = jnp.dot(scaled, spread, precision=HIGHEST, preferred_element_type=jnp.float32)
        for j in range(NJ):
            pot[x, j] = wide[:, 128 * j : 128 * (j + 1)]
        return carry

    pl.semaphore_wait(barrier, count)

    def sections(dim):
        sizes = ((XO, CX, 6), (JO, NJ, 2), (YO, CY, 8))
        axis = (0, 2, 1)[dim]
        start, extent, depth = sizes[axis]
        picks = []
        for at in (start, start + extent - depth, start - depth, start + extent):
            index = list(OWN)
            index[axis] = pl.ds(at, depth)
            picks.append(tuple(index))
        return picks

    def halo(field, step):
        copies = []
        for dim, (stride, at, n) in enumerate(faces):
            low_rim, high_rim, below, above = sections(dim)
            up = pltpu.make_async_remote_copy(
                field.at[high_rim],
                field.at[below],
                hs.at[step, 2 * dim],
                hr.at[step, 2 * dim],
                device_id=(lax.rem(dom + stride, 128), band),
                device_id_type=MESH,
            )
            down = pltpu.make_async_remote_copy(
                field.at[low_rim],
                field.at[above],
                hs.at[step, 2 * dim + 1],
                hr.at[step, 2 * dim + 1],
                device_id=(lax.rem(dom - stride + 128, 128), band),
                device_id_type=MESH,
            )
            copies.append((up, at < n - 1, at > 0, below))
            copies.append((down, at > 0, at < n - 1, above))
        return copies

    def start(copies, field):
        for copy, sends, receives, landing in copies:

            @pl.when(sends)
            def _():
                copy.start()

        for copy, sends, receives, landing in copies:

            @pl.when(jnp.logical_not(receives))
            def _():
                xs, js, ys = landing

                def clear(i, carry):
                    field[xs.start + i, js, ys] = jnp.zeros((js.size, ys.size, 128), jnp.float32)
                    return carry

                lax.fori_loop(0, xs.size, clear, 0)

    def arrive(copies):
        for copy, sends, receives, landing in copies:

            @pl.when(receives)
            def _():
                copy.wait_recv()

    def drain(copies):
        for copy, sends, receives, landing in copies:

            @pl.when(sends)
            def _():
                copy.wait_send()

    for copy in loads:
        copy.wait()
    first = halo(e0, 0)
    start(first, e0)
    lax.fori_loop(0, CX, spread_pot, 0)
    arrive(first)

    def step_one(x, carry):
        for j, value in enumerate(stencil(e0, pot, x)):
            e1[XO + x, JO + j, pl.ds(YO, CY), :] = value
        return carry

    lax.fori_loop(0, CX, step_one, 0)
    second = halo(e1, 1)
    start(second, e1)
    arrive(second)

    def step_two(x, carry):
        for j, value in enumerate(stencil(e1, pot, x)):
            own = e0[XO + x, JO + j, pl.ds(YO, CY), :]
            e2[XO + x, JO + j, pl.ds(YO, CY), :] = 2.0 * value - own
        return carry

    lax.fori_loop(0, CX, step_two, 0)
    third = halo(e2, 2)
    start(third, e2)
    over = pltpu.make_async_remote_copy(
        e2.at[OWN], other, bs, br, device_id=(dom, 1 - band), device_id_type=MESH
    )

    @pl.when(band == 0)
    def _():
        over.start()

    keep = pltpu.make_async_copy(e2.at[OWN], filt_ref, load_sem.at[0])
    keep.start()
    drain(first)
    drain(second)
    arrive(third)

    def step_three(x, carry):
        for j, value in enumerate(stencil(e2, pot, x)):
            img[x, j] = value
        return carry

    lax.fori_loop(0, CX, step_three, 0)

    @pl.when(band == 1)
    def _():
        over.wait_recv()

    def gram(left):
        def add(x, acc):
            rows = left(x)
            own = e2[XO + x, pl.ds(JO, NJ), pl.ds(YO, CY), :].reshape(NJ * CY, 128)
            both = jnp.concatenate([own, img[x].reshape(NJ * CY, 128)], axis=1)
            return acc + lax.dot_general(
                rows,
                both,
                (((0,), (0,)), ((), ())),
                precision=HIGHEST,
                preferred_element_type=jnp.float32,
            )

        acc = lax.fori_loop(0, CX, add, jnp.zeros((128, 256), jnp.float32))
        blocks = []
        for half in range(2):
            total = acc[:OB, 128 * half : 128 * half + OB]
            for g in range(1, 4):
                total = total + acc[OB * g : OB * (g + 1), 128 * half + OB * g : 128 * half + OB * (g + 1)]
            blocks.append(total)
        return blocks

    part[...] = jnp.zeros_like(part)

    @pl.when(band == 0)
    def _():
        corr, ham = gram(
            lambda x: e2[XO + x, pl.ds(JO, NJ), pl.ds(YO, CY), :].reshape(NJ * CY, 128)
        )
        part[0, 0, :, 0:OB] = corr
        part[0, 0, :, 2 * OB : 3 * OB] = ham

    @pl.when(band == 1)
    def _():
        corr, ham = gram(
            lambda x: e2[XO + x, pl.ds(JO, NJ), pl.ds(YO, CY), :].reshape(NJ * CY, 128)
        )
        part[0, 1, :, OB : 2 * OB] = corr
        part[0, 1, :, 3 * OB : 4 * OB] = ham
        corr, ham = gram(lambda x: other[x].reshape(NJ * CY, 128))
        part[0, 0, :, OB : 2 * OB] = corr
        part[0, 0, :, 3 * OB : 4 * OB] = ham

    keep.wait()
    back = pltpu.make_async_copy(other, band_ref, load_sem.at[1])

    @pl.when(band == 1)
    def _():
        back.start()

    def exchange(source, targets, slot):
        copies = []
        for k, peer in enumerate(targets):
            copy = pltpu.make_async_remote_copy(
                source,
                recv.at[slot + k],
                rs.at[slot + k],
                rr.at[slot + k],
                device_id=peer,
                device_id_type=MESH,
            )
            copy.start()
            copies.append(copy)
        for copy in copies:
            copy.wait()

    exchange(part.at[0, 1 - core], [peers[0]], 0)
    part[1, 0] = part[0, core] + recv[0]
    exchange(part.at[1, 0], [peers[1]], 1)
    part[1, 1] = part[1, 0] + recv[1]
    exchange(part.at[1, 1], zpeers, 2)
    part[2, 0] = part[1, 1] + recv[2] + recv[3] + recv[4]
    exchange(part.at[2, 0], ypeers, 5)
    part[2, 1] = part[2, 0] + recv[5] + recv[6] + recv[7]
    exchange(part.at[2, 1], xpeers, 8)
    part[3, 0] = part[2, 1] + recv[8] + recv[9] + recv[10]
    exchange(part.at[3, 0], [peers[0]], 11)
    mats_ref[core] = part[3, 0]
    mats_ref[1 - core] = recv[11]

    drain(third)

    @pl.when(band == 0)
    def _():
        over.wait_send()

    @pl.when(band == 1)
    def _():
        back.wait()


def run_filter(orbitals, potential):
    big = (XO * 2 + CX, JO * 2 + NJ, YO * 2 + CY, 128)
    tile = (CX, NJ, CY, 128)
    vmem = pl.BlockSpec(memory_space=pltpu.VMEM)
    hbm = pl.BlockSpec(memory_space=pl.ANY)
    f32 = jnp.float32
    dma = pltpu.SemaphoreType.DMA
    return pl.pallas_call(
        filter_kernel,
        out_shape=(
            jax.ShapeDtypeStruct(tile, f32),
            jax.ShapeDtypeStruct(tile, f32),
            jax.ShapeDtypeStruct((2, OB, 128), f32),
        ),
        in_specs=[hbm, vmem],
        out_specs=(hbm, hbm, vmem),
        scratch_shapes=[
            pltpu.VMEM(big, f32),
            pltpu.VMEM(big, f32),
            pltpu.VMEM(big, f32),
            pltpu.VMEM(tile, f32),
            pltpu.VMEM(tile, f32),
            pltpu.VMEM(tile, f32),
            pltpu.VMEM((4, 2, OB, 128), f32),
            pltpu.VMEM((12, OB, 128), f32),
            dma((NJ,)),
            dma((3, 6)),
            dma((3, 6)),
            dma,
            dma,
            dma((12,)),
            dma((12,)),
        ],
        compiler_params=pltpu.CompilerParams(
            collective_id=0, has_side_effects=True, vmem_limit_bytes=48 << 20
        ),
    )(orbitals, potential)


def rotate_kernel(own_ref, other_ref, coef_ref, out_ref):
    band = lax.axis_index("band")
    own = own_ref[...].reshape(CX * CY, 128)
    mine = jnp.dot(own, coef_ref[0], precision=HIGHEST, preferred_element_type=jnp.float32)

    @pl.when(band == 0)
    def _():
        out_ref[0, 0] = mine.reshape(CX, CY, 128)

    @pl.when(band == 1)
    def _():
        rest = other_ref[...].reshape(CX * CY, 128)
        total = mine + jnp.dot(
            rest, coef_ref[1], precision=HIGHEST, preferred_element_type=jnp.float32
        )
        out_ref[0, 0] = total.reshape(CX, CY, 128)


def rotate(own, other, coef):
    spec = pl.BlockSpec((CX, 1, CY, 128), lambda j: (0, j, 0, 0))
    return pl.pallas_call(
        rotate_kernel,
        out_shape=jax.ShapeDtypeStruct((1, 1, CX, CY, CZ * OB), jnp.float32),
        grid=(NJ,),
        in_specs=[spec, spec, pl.BlockSpec((2, 128, 128), lambda j: (0, 0, 0))],
        out_specs=pl.BlockSpec((1, 1, CX, CY, 128), lambda j: (0, 0, 0, 0, j)),
    )(own, other, coef)


def local(orbitals, potential):
    filt, other, mats = run_filter(orbitals, potential)
    mats = mats.reshape(2 * OB, 128) / CELLS
    corr, ham = mats[:, : 2 * OB], mats[:, 2 * OB :]

    def whole(m):
        return jnp.block([[m[:OB, :OB], m[:OB, OB:]], [m[:OB, OB:].T, m[OB:, OB:]]])

    corr, ham = whole(corr), whole(ham)
    lower = jnp.linalg.cholesky(corr)
    inverse = lax.linalg.triangular_solve(
        lower, jnp.eye(2 * OB, dtype=jnp.float32), left_side=True, lower=True
    )
    projected = jnp.dot(jnp.dot(inverse, ham, precision=HIGHEST), inverse.T, precision=HIGHEST)
    band = lax.axis_index("band")
    rows = lax.dynamic_slice_in_dim(inverse, band * OB, OB, 0)
    mine = lax.dynamic_slice_in_dim(rows, band * OB, OB, 1).T
    rest = rows[:, :OB].T
    eye = jnp.eye(4, dtype=jnp.float32)
    coef = jnp.stack([jnp.kron(eye, mine), jnp.kron(eye, rest)])
    return rotate(filt, other, coef), projected


def solution(mesh):
    return jax.shard_map(
        local,
        mesh=mesh,
        in_specs=(P("dom", "band", None, None, None), P("dom", None, None, None)),
        out_specs=(P("dom", "band", None, None, None), P()),
        check_vma=False,
    )
```

```python
import functools

import jax
import jax.numpy as jnp
from jax import lax
from jax.experimental import pallas as pl
from jax.experimental.pallas import tpu as pltpu
from jax.sharding import PartitionSpec as P

COEFFS = (
    -5369.0 / 1800.0,
    12.0 / 7.0,
    -15.0 / 56.0,
    10.0 / 189.0,
    -1.0 / 112.0,
    2.0 / 1925.0,
    -1.0 / 16632.0,
)
SPACING = 0.32
CENTER = 71.0
HALFWIDTH = 69.0
KINETIC = -0.5 / SPACING**2 / HALFWIDTH
A = tuple(KINETIC * c for c in COEFFS)

CX, CY, CZ, OB = 12, 32, 32, 32
PX, PY, PZ = 8, 4, 4
NJ = CZ * OB // 128
CELLS = PX * CX * PY * CY * PZ * CZ
MESH = pl.DeviceIdType.MESH
HIGHEST = lax.Precision.HIGHEST
XO, JO, YO = 6, 2, 8
OWN = (pl.ds(XO, CX), pl.ds(JO, NJ), pl.ds(YO, CY))


def stencil(field, pot, x):
    lane = lax.broadcasted_iota(jnp.int32, (CY, 128), 1)

    def tile(j, dx=0, dy=0):
        return field[XO + x + dx, JO + j, pl.ds(YO + dy, CY), :]

    def partial(j):
        m2, m1, v, p1 = tile(j - 2), tile(j - 1), tile(j), tile(j + 1)
        t1 = A[3] * m1 + A[1] * v + A[5] * p1
        t2 = A[2] * (v + m1) + A[6] * (p1 + m2)
        t3 = A[3] * v + A[1] * m1 + A[5] * m2
        return (
            pltpu.roll(t1, 96, 1),
            pltpu.roll(t2, 64, 1),
            pltpu.roll(t3, 32, 1),
        )

    out = []
    low = partial(0)
    for j in range(NJ):
        high = partial(j + 1)
        acc = jnp.where(lane < 96, low[0], high[0])
        acc = acc + jnp.where(lane < 64, low[1], high[1])
        acc = acc + jnp.where(lane < 32, low[2], high[2])
        low = high
        acc = acc + pot[x, j] * tile(j)
        for k in range(1, 7):
            terms = tile(j, k) + tile(j, -k) + tile(j, 0, k) + tile(j, 0, -k)
            if k == 4:
                terms = terms + (tile(j + 1) + tile(j - 1))
            acc = acc + A[k] * terms
        out.append(acc)
    return out


def filter_kernel(
    orb_ref,
    pot_ref,
    out_ref,
    proj_ref,
    e0,
    e1,
    e2,
    img,
    pot,
    other,
    part,
    recv,
    work,
    coef,
    load_sem,
    hs,
    hr,
    bs,
    br,
    rs,
    rr,
):
    dom = lax.axis_index("dom")
    band = lax.axis_index("band")
    tz = lax.rem(dom, PZ)
    ty = lax.rem(dom // PZ, PY)
    tx = dom // (PY * PZ)
    px, py, pz, core = dom // 32, lax.rem(dom // 8, 4), lax.rem(dom // 2, 4), lax.rem(dom, 2)

    loads = [
        pltpu.make_async_copy(
            orb_ref.at[0, 0, :, :, pl.ds(128 * j, 128)],
            e0.at[pl.ds(XO, CX), JO + j, pl.ds(YO, CY)],
            load_sem.at[j],
        )
        for j in range(NJ)
    ]
    for copy in loads:
        copy.start()

    def place(x, y, z, c):
        return ((x * 4 + y) * 4 + z) * 2 + c

    faces = (
        (PY * PZ, tx, PX),
        (PZ, ty, PY),
        (1, tz, PZ),
    )
    twin = (place(px, py, pz, 1 - core), band)
    column = [
        (place(px, py, lax.rem(pz + k, 4), core), lax.rem(band + b, 2))
        for k in range(4)
        for b in range(2)
        if k or b
    ]
    plane = [
        (place(lax.rem(px + i, 4), lax.rem(py + k, 4), pz, core), band)
        for i in range(4)
        for k in range(4)
        if i or k
    ]
    stages = ((twin,), column, plane, (twin,))
    slots = (0, 1, 8, 23)

    barrier = pltpu.get_barrier_semaphore()
    count = jnp.int32(23)
    for peer in [twin] + column + plane:
        pl.semaphore_signal(barrier, inc=1, device_id=peer, device_id_type=MESH)
    for stride, at, n in faces:
        has_low, has_high = at > 0, at < n - 1
        count = count + has_low.astype(jnp.int32) + has_high.astype(jnp.int32)

        @pl.when(has_low)
        def _():
            pl.semaphore_signal(barrier, inc=1, device_id=(dom - stride, band), device_id_type=MESH)

        @pl.when(has_high)
        def _():
            pl.semaphore_signal(barrier, inc=1, device_id=(dom + stride, band), device_id_type=MESH)

    row = lax.broadcasted_iota(jnp.int32, (CZ, CZ * OB), 0)
    col = lax.broadcasted_iota(jnp.int32, (CZ, CZ * OB), 1)
    spread = (row == col // OB).astype(jnp.float32)

    def spread_pot(x, carry):
        scaled = (pot_ref[0, x] - CENTER) * (1.0 / HALFWIDTH) + 3.0 * A[0]
        wide = jnp.dot(scaled, spread, precision=HIGHEST, preferred_element_type=jnp.float32)
        for j in range(NJ):
            pot[x, j] = wide[:, 128 * j : 128 * (j + 1)]
        return carry

    pl.semaphore_wait(barrier, count)

    def sections(dim):
        sizes = ((XO, CX, 6), (JO, NJ, 2), (YO, CY, 6))
        axis = (0, 2, 1)[dim]
        start, extent, depth = sizes[axis]
        picks = []
        for at in (start, start + extent - depth, start - depth, start + extent):
            index = list(OWN)
            index[axis] = pl.ds(at, depth)
            picks.append(tuple(index))
        return picks

    def halo(field, step):
        copies = []
        for dim, (stride, at, n) in enumerate(faces):
            low_rim, high_rim, below, above = sections(dim)
            up = pltpu.make_async_remote_copy(
                field.at[high_rim],
                field.at[below],
                hs.at[step, 2 * dim],
                hr.at[step, 2 * dim],
                device_id=(lax.rem(dom + stride, 128), band),
                device_id_type=MESH,
            )
            down = pltpu.make_async_remote_copy(
                field.at[low_rim],
                field.at[above],
                hs.at[step, 2 * dim + 1],
                hr.at[step, 2 * dim + 1],
                device_id=(lax.rem(dom - stride + 128, 128), band),
                device_id_type=MESH,
            )
            copies.append((up, at < n - 1, at > 0, below))
            copies.append((down, at > 0, at < n - 1, above))
        return copies

    def start(copies, field):
        for copy, sends, receives, landing in copies:

            @pl.when(sends)
            def _():
                copy.start()

        for copy, sends, receives, landing in copies:

            @pl.when(jnp.logical_not(receives))
            def _():
                xs, js, ys = landing

                def clear(i, carry):
                    field[xs.start + i, js, ys] = jnp.zeros((js.size, ys.size, 128), jnp.float32)
                    return carry

                lax.fori_loop(0, xs.size, clear, 0)

    def arrive(copies):
        for copy, sends, receives, landing in copies:

            @pl.when(receives)
            def _():
                copy.wait_recv()

    def drain(copies):
        for copy, sends, receives, landing in copies:

            @pl.when(sends)
            def _():
                copy.wait_send()

    for copy in loads:
        copy.wait()
    first = halo(e0, 0)
    start(first, e0)
    lax.fori_loop(0, CX, spread_pot, 0)
    arrive(first)

    def step_one(x, carry):
        for j, value in enumerate(stencil(e0, pot, x)):
            e1[XO + x, JO + j, pl.ds(YO, CY), :] = value
        return carry

    lax.fori_loop(0, CX, step_one, 0)
    second = halo(e1, 1)
    start(second, e1)
    arrive(second)

    def step_two(x, carry):
        for j, value in enumerate(stencil(e1, pot, x)):
            own = e0[XO + x, JO + j, pl.ds(YO, CY), :]
            e2[XO + x, JO + j, pl.ds(YO, CY), :] = 2.0 * value - own
        return carry

    lax.fori_loop(0, CX, step_two, 0)
    low, high = pl.ds(0, CX // 2), pl.ds(CX // 2, CX // 2)
    partner = (dom, 1 - band)

    def across(planes, at):
        return pltpu.make_async_remote_copy(
            e2.at[pl.ds(XO + planes.start, planes.size), OWN[1], OWN[2]],
            other.at[planes],
            bs.at[at],
            br.at[at],
            device_id=partner,
            device_id_type=MESH,
        )

    upper, lower, rest = across(high, 0), across(low, 1), across(low, 2)

    @pl.when(band == 0)
    def _():
        upper.start()

    @pl.when(band == 1)
    def _():
        lower.start()

    third = halo(e2, 2)
    start(third, e2)

    def own(x):
        return e2[XO + x, pl.ds(JO, NJ), pl.ds(YO, CY), :].reshape(NJ * CY, 128)

    def theirs(x):
        return other[x].reshape(NJ * CY, 128)

    def image(x):
        return img[x].reshape(NJ * CY, 128)

    def gram(left, right, begin, end):
        def add(x, acc):
            return acc + lax.dot_general(
                left(x),
                right(x),
                (((0,), (0,)), ((), ())),
                precision=HIGHEST,
                preferred_element_type=jnp.float32,
            )

        acc = lax.fori_loop(begin, end, add, jnp.zeros((128, 128), jnp.float32))
        total = acc[:OB, :OB]
        for g in range(1, 4):
            total = total + acc[OB * g : OB * (g + 1), OB * g : OB * (g + 1)]
        return total

    def stage_copies(which, n):
        source = part.at[which, 0, 1 - core] if n == 0 else part.at[which, n, 0]
        return [
            pltpu.make_async_remote_copy(
                source,
                recv.at[which, slots[n] + k],
                rs.at[which, slots[n] + k],
                rr.at[which, slots[n] + k],
                device_id=peer,
                device_id_type=MESH,
            )
            for k, peer in enumerate(stages[n])
        ]

    def send(which, n):
        copies = stage_copies(which, n)
        for copy in copies:
            copy.start()
        return copies

    def collect(which, n, copies):
        for copy in copies:
            copy.wait()
        total = part[which, 0, core] if n == 0 else part[which, n, 0]
        if n == 3:
            part[which, 0, core] = total
            part[which, 0, 1 - core] = recv[which, slots[3]]
            return
        for k in range(len(copies)):
            total = total + recv[which, slots[n] + k]
        part[which, n + 1, 0] = total

    def put(which, column, block):
        for half in range(2):
            part[which, 0, half, :, OB * column : OB * (column + 1)] = block[
                half * (OB // 2) : (half + 1) * (OB // 2)
            ]

    part[...] = jnp.zeros_like(part)
    mine = gram(own, own, 0, CX)

    @pl.when(band == 0)
    def _():
        put(0, 0, mine)
        upper.wait_send()
        rest.start()
        lower.wait_recv()
        put(0, 1, gram(own, theirs, 0, CX // 2))

    @pl.when(band == 1)
    def _():
        put(0, 2, mine)
        upper.wait_recv()
        put(0, 1, gram(theirs, own, CX // 2, CX))

    for n in range(4):
        collect(0, n, send(0, n))

    eye = (
        lax.broadcasted_iota(jnp.int32, (OB, OB), 0) == lax.broadcasted_iota(jnp.int32, (OB, OB), 1)
    ).astype(jnp.float32)

    def matrix(which, dst):
        blocks = part[which, 0].reshape(OB, 128) * (1.0 / CELLS)
        cross = blocks[:, OB : 2 * OB]
        dst[0:OB, 0:OB] = blocks[:, 0:OB]
        dst[0:OB, OB : 2 * OB] = cross
        dst[OB : 2 * OB, OB : 2 * OB] = blocks[:, 2 * OB : 3 * OB]
        dst[OB : 2 * OB, 0:OB] = lax.dot_general(
            cross,
            eye,
            (((0,), (0,)), ((), ())),
            precision=HIGHEST,
            preferred_element_type=jnp.float32,
        )

    n_orb = 2 * OB
    row_id = lax.broadcasted_iota(jnp.int32, (n_orb, 128), 0)
    lane_id = lax.broadcasted_iota(jnp.int32, (n_orb, 128), 1)
    work[0] = (lane_id == row_id + n_orb).astype(jnp.float32)
    matrix(0, work.at[0])

    def eliminate(k, m):
        pivot_row = jnp.sum(jnp.where(row_id == k, m, 0.0), axis=0, keepdims=True)
        pivot_col = jnp.sum(jnp.where(lane_id == k, m, 0.0), axis=1, keepdims=True)
        pivot = jnp.sum(jnp.where(lane_id[:1] == k, pivot_row, 0.0), axis=1, keepdims=True)
        factor = jnp.where(row_id > k, pivot_col * (1.0 / pivot), 0.0)
        return m - factor * pivot_row

    m = lax.fori_loop(0, n_orb, eliminate, work[0])
    diag = jnp.sum(jnp.where(lane_id == row_id, m, 0.0), axis=1, keepdims=True)
    inverse = m * (1.0 / jnp.sqrt(diag))
    work[0] = inverse

    src = lax.broadcasted_iota(jnp.int32, (128, 128), 0)
    dst = lax.broadcasted_iota(jnp.int32, (128, 128), 1)
    same = src // OB == dst // OB
    mine_rows = work[0, pl.ds(pl.multiple_of(band * OB, OB), OB), :]

    def weights(column):
        pick = (src == n_orb + OB * column + lax.rem(dst, OB)).astype(jnp.float32)
        wide = jnp.dot(mine_rows, pick, precision=HIGHEST, preferred_element_type=jnp.float32)
        return jnp.where(same, jnp.concatenate([wide] * 4, axis=0), 0.0)

    coef[0] = weights(band)
    coef[1] = weights(0)

    arrive(third)

    def step_three(x, carry):
        for j, value in enumerate(stencil(e2, pot, x)):
            img[x, j] = value
        return carry

    lax.fori_loop(0, CX, step_three, 0)
    ham = gram(own, image, 0, CX)

    @pl.when(band == 0)
    def _():
        put(1, 0, ham)

    @pl.when(band == 1)
    def _():
        put(1, 2, ham)
        rest.wait_recv()
        put(1, 1, gram(theirs, image, 0, CX))

    def turn(x, carry):
        def times(rows, w):
            return lax.dot_general(
                rows,
                w,
                (((1,), (1,)), ((), ())),
                precision=HIGHEST,
                preferred_element_type=jnp.float32,
            )

        img[x] = times(own(x), coef[0]).reshape(NJ, CY, 128)

        @pl.when(band == 1)
        def _():
            img[x] = img[x] + times(theirs(x), coef[1]).reshape(NJ, CY, 128)

        return carry

    bounds = (0, 2, 7, 12, 12)
    for n in range(4):
        copies = send(1, n)
        lax.fori_loop(bounds[n], bounds[n + 1], turn, 0)
        if n == 3:
            stores = [
                pltpu.make_async_copy(
                    img.at[:, j], out_ref.at[0, 0, :, :, pl.ds(128 * j, 128)], load_sem.at[j]
                )
                for j in range(NJ)
            ]
            for copy in stores:
                copy.start()
        collect(1, n, copies)

    matrix(1, work.at[1])
    pick = (
        lax.broadcasted_iota(jnp.int32, (128, n_orb), 0)
        == n_orb + lax.broadcasted_iota(jnp.int32, (128, n_orb), 1)
    ).astype(jnp.float32)
    inv = jnp.dot(work[0], pick, precision=HIGHEST, preferred_element_type=jnp.float32)
    left = jnp.dot(
        inv, work[1, :, 0:n_orb], precision=HIGHEST, preferred_element_type=jnp.float32
    )
    proj_ref[...] = lax.dot_general(
        left,
        inv,
        (((1,), (1,)), ((), ())),
        precision=HIGHEST,
        preferred_element_type=jnp.float32,
    )
    for copy in stores:
        copy.wait()
    drain(first)
    drain(second)
    drain(third)

    @pl.when(band == 0)
    def _():
        rest.wait_send()

    @pl.when(band == 1)
    def _():
        lower.wait_send()


def local(orbitals, potential):
    big = (XO * 2 + CX, JO * 2 + NJ, YO * 2 + CY, 128)
    tile = (CX, NJ, CY, 128)
    vmem = pl.BlockSpec(memory_space=pltpu.VMEM)
    hbm = pl.BlockSpec(memory_space=pl.ANY)
    f32 = jnp.float32
    dma = pltpu.SemaphoreType.DMA
    return pl.pallas_call(
        filter_kernel,
        out_shape=(
            jax.ShapeDtypeStruct((1, 1, CX, CY, CZ * OB), f32),
            jax.ShapeDtypeStruct((2 * OB, 2 * OB), f32),
        ),
        in_specs=[hbm, vmem],
        out_specs=(hbm, vmem),
        scratch_shapes=[
            pltpu.VMEM(big, f32),
            pltpu.VMEM(big, f32),
            pltpu.VMEM(big, f32),
            pltpu.VMEM(tile, f32),
            pltpu.VMEM(tile, f32),
            pltpu.VMEM(tile, f32),
            pltpu.VMEM((2, 4, 2, OB // 2, 128), f32),
            pltpu.VMEM((2, 24, OB // 2, 128), f32),
            pltpu.VMEM((2, 2 * OB, 128), f32),
            pltpu.VMEM((2, 128, 128), f32),
            dma((NJ,)),
            dma((3, 6)),
            dma((3, 6)),
            dma((3,)),
            dma((3,)),
            dma((2, 24)),
            dma((2, 24)),
        ],
        compiler_params=pltpu.CompilerParams(
            collective_id=0, has_side_effects=True, vmem_limit_bytes=48 << 20
        ),
    )(orbitals, potential)


def solution(mesh):
    return jax.shard_map(
        local,
        mesh=mesh,
        in_specs=(P("dom", "band", None, None, None), P("dom", None, None, None)),
        out_specs=(P("dom", "band", None, None, None), P()),
        check_vma=False,
    )
```

```python
import functools

import jax
import jax.numpy as jnp
from jax import lax
from jax.experimental import pallas as pl
from jax.experimental.pallas import tpu as pltpu
from jax.sharding import PartitionSpec as P

COEFFS = (
    -5369.0 / 1800.0,
    12.0 / 7.0,
    -15.0 / 56.0,
    10.0 / 189.0,
    -1.0 / 112.0,
    2.0 / 1925.0,
    -1.0 / 16632.0,
)
SPACING = 0.32
CENTER = 71.0
HALFWIDTH = 69.0
KINETIC = -0.5 / SPACING**2 / HALFWIDTH
A = tuple(KINETIC * c for c in COEFFS)

CX, CY, CZ, OB = 12, 32, 32, 32
PX, PY, PZ = 8, 4, 4
NJ = CZ * OB // 128
CELLS = PX * CX * PY * CY * PZ * CZ
MESH = pl.DeviceIdType.MESH
HIGHEST = lax.Precision.HIGHEST
XO, JO, YO = 6, 2, 8
OWN = (pl.ds(XO, CX), pl.ds(JO, NJ), pl.ds(YO, CY))


def stencil(field, pot, x):
    lane = lax.broadcasted_iota(jnp.int32, (CY, 128), 1)

    def tile(j, dx=0, dy=0):
        return field[XO + x + dx, JO + j, pl.ds(YO + dy, CY), :]

    def partial(j):
        m2, m1, v, p1 = tile(j - 2), tile(j - 1), tile(j), tile(j + 1)
        t1 = A[3] * m1 + A[1] * v + A[5] * p1
        t2 = A[2] * (v + m1) + A[6] * (p1 + m2)
        t3 = A[3] * v + A[1] * m1 + A[5] * m2
        return (
            pltpu.roll(t1, 96, 1),
            pltpu.roll(t2, 64, 1),
            pltpu.roll(t3, 32, 1),
        )

    out = []
    low = partial(0)
    for j in range(NJ):
        high = partial(j + 1)
        acc = jnp.where(lane < 96, low[0], high[0])
        acc = acc + jnp.where(lane < 64, low[1], high[1])
        acc = acc + jnp.where(lane < 32, low[2], high[2])
        low = high
        acc = acc + pot[x, j] * tile(j)
        for k in range(1, 7):
            terms = tile(j, k) + tile(j, -k) + tile(j, 0, k) + tile(j, 0, -k)
            if k == 4:
                terms = terms + (tile(j + 1) + tile(j - 1))
            acc = acc + A[k] * terms
        out.append(acc)
    return out


def forward_stencil(field, pot, x):
    lane = lax.broadcasted_iota(jnp.int32, (CY, 128), 1)

    def tile(j, dx=0, dy=0):
        return field[XO + x + dx, JO + j, pl.ds(YO + dy, CY), :]

    def partial(j):
        v, p1 = tile(j), tile(j + 1)
        return (
            pltpu.roll(A[1] * v + A[5] * p1, 96, 1),
            pltpu.roll(A[2] * v + A[6] * p1, 64, 1),
            pltpu.roll(A[3] * v, 32, 1),
        )

    out = []
    low = partial(0)
    for j in range(NJ):
        high = partial(j + 1)
        acc = jnp.where(lane < 96, low[0], high[0])
        acc = acc + jnp.where(lane < 64, low[1], high[1])
        acc = acc + jnp.where(lane < 32, low[2], high[2])
        low = high
        acc = acc + 0.5 * pot[x, j] * tile(j)
        for k in range(1, 7):
            terms = tile(j, k) + tile(j, 0, k)
            if k == 4:
                terms = terms + tile(j + 1)
            acc = acc + A[k] * terms
        out.append(acc)
    return out


def filter_kernel(
    orb_ref,
    pot_hbm,
    out_ref,
    proj_ref,
    e0,
    e1,
    e2,
    img,
    pot,
    other,
    part,
    recv,
    work,
    coef,
    pot_ref,
    load_sem,
    out_sem,
    hs,
    hr,
    bs,
    br,
    rs,
    rr,
):
    dom = lax.axis_index("dom")
    band = lax.axis_index("band")
    tz = lax.rem(dom, PZ)
    ty = lax.rem(dom // PZ, PY)
    tx = dom // (PY * PZ)
    px, py, pz, core = dom // 32, lax.rem(dom // 8, 4), lax.rem(dom // 2, 4), lax.rem(dom, 2)

    loads = [
        pltpu.make_async_copy(
            orb_ref.at[0, 0, :, :, pl.ds(128 * j, 128)],
            e0.at[pl.ds(XO, CX), JO + j, pl.ds(YO, CY)],
            load_sem.at[j],
        )
        for j in range(NJ)
    ]
    loads.append(pltpu.make_async_copy(pot_hbm, pot_ref, load_sem.at[NJ]))
    for copy in loads:
        copy.start()

    def place(x, y, z, c):
        return ((x * 4 + y) * 4 + z) * 2 + c

    faces = (
        (PY * PZ, tx, PX),
        (PZ, ty, PY),
        (1, tz, PZ),
    )
    twin = (place(px, py, pz, 1 - core), band)
    column = [
        (place(px, py, lax.rem(pz + k, 4), core), lax.rem(band + b, 2))
        for k in range(4)
        for b in range(2)
        if k or b
    ]
    plane = [
        (place(lax.rem(px + i, 4), lax.rem(py + k, 4), pz, core), band)
        for i in range(4)
        for k in range(4)
        if i or k
    ]
    stages = ((twin,), column, plane, (twin,))
    slots = (0, 1, 8, 23)

    barrier = pltpu.get_barrier_semaphore()
    count = jnp.int32(23)
    for peer in [twin] + column + plane:
        pl.semaphore_signal(barrier, inc=1, device_id=peer, device_id_type=MESH)
    for stride, at, n in faces:
        has_low, has_high = at > 0, at < n - 1
        count = count + has_low.astype(jnp.int32) + has_high.astype(jnp.int32)

        @pl.when(has_low)
        def _():
            pl.semaphore_signal(barrier, inc=1, device_id=(dom - stride, band), device_id_type=MESH)

        @pl.when(has_high)
        def _():
            pl.semaphore_signal(barrier, inc=1, device_id=(dom + stride, band), device_id_type=MESH)

    row = lax.broadcasted_iota(jnp.int32, (CZ, CZ * OB), 0)
    col = lax.broadcasted_iota(jnp.int32, (CZ, CZ * OB), 1)
    spread = (row == col // OB).astype(jnp.float32)

    def spread_pot(x, carry):
        scaled = (pot_ref[0, x] - CENTER) * (1.0 / HALFWIDTH) + 3.0 * A[0]
        wide = jnp.dot(scaled, spread, precision=HIGHEST, preferred_element_type=jnp.float32)
        for j in range(NJ):
            pot[x, j] = wide[:, 128 * j : 128 * (j + 1)]
        return carry

    pl.semaphore_wait(barrier, count)

    def sections(dim):
        sizes = ((XO, CX, 6), (JO, NJ, 2), (YO, CY, 6))
        axis = (0, 2, 1)[dim]
        start, extent, depth = sizes[axis]
        picks = []
        for at in (start, start + extent - depth, start - depth, start + extent):
            index = list(OWN)
            index[axis] = pl.ds(at, depth)
            picks.append(tuple(index))
        return picks

    def halo(field, step):
        copies = []
        for dim, (stride, at, n) in enumerate(faces):
            low_rim, high_rim, below, above = sections(dim)
            up = pltpu.make_async_remote_copy(
                field.at[high_rim],
                field.at[below],
                hs.at[step, 2 * dim],
                hr.at[step, 2 * dim],
                device_id=(lax.rem(dom + stride, 128), band),
                device_id_type=MESH,
            )
            down = pltpu.make_async_remote_copy(
                field.at[low_rim],
                field.at[above],
                hs.at[step, 2 * dim + 1],
                hr.at[step, 2 * dim + 1],
                device_id=(lax.rem(dom - stride + 128, 128), band),
                device_id_type=MESH,
            )
            copies.append((up, at < n - 1, at > 0, below))
            copies.append((down, at > 0, at < n - 1, above))
        return copies

    def start(copies, field):
        for copy, sends, receives, landing in copies:

            @pl.when(sends)
            def _():
                copy.start()

        for copy, sends, receives, landing in copies:

            @pl.when(jnp.logical_not(receives))
            def _():
                xs, js, ys = landing

                def clear(i, carry):
                    field[xs.start + i, js, ys] = jnp.zeros((js.size, ys.size, 128), jnp.float32)
                    return carry

                lax.fori_loop(0, xs.size, clear, 0)

    def arrive(copies):
        for copy, sends, receives, landing in copies:

            @pl.when(receives)
            def _():
                copy.wait_recv()

    def drain(copies):
        for copy, sends, receives, landing in copies:

            @pl.when(sends)
            def _():
                copy.wait_send()

    for copy in loads:
        copy.wait()
    first = halo(e0, 0)
    start(first, e0)
    lax.fori_loop(0, CX, spread_pot, 0)
    arrive(first)

    def step_one(x, carry):
        for j, value in enumerate(stencil(e0, pot, x)):
            e1[XO + x, JO + j, pl.ds(YO, CY), :] = value
        return carry

    lax.fori_loop(0, CX, step_one, 0)
    second = halo(e1, 1)
    start(second, e1)
    arrive(second)

    def step_two(x, carry):
        for j, value in enumerate(stencil(e1, pot, x)):
            own = e0[XO + x, JO + j, pl.ds(YO, CY), :]
            e2[XO + x, JO + j, pl.ds(YO, CY), :] = 2.0 * value - own
        return carry

    lax.fori_loop(0, CX, step_two, 0)
    third = halo(e2, 2)[1::2]
    start(third, e2)
    partner = (dom, 1 - band)
    parts = (pl.ds(0, CX // 2), pl.ds(CX // 2, CX // 2))
    across = [
        pltpu.make_async_remote_copy(
            e2.at[pl.ds(XO + planes.start, planes.size), OWN[1], OWN[2]],
            other.at[planes],
            bs.at[at],
            br.at[at],
            device_id=partner,
            device_id_type=MESH,
        )
        for at, planes in enumerate(parts)
    ]
    for copy in across:
        copy.start()

    def own(x):
        return e2[XO + x, pl.ds(JO, NJ), pl.ds(YO, CY), :].reshape(NJ * CY, 128)

    def theirs(x):
        return other[x].reshape(NJ * CY, 128)

    def image(x):
        return img[x].reshape(NJ * CY, 128)

    def gram(left, right, begin, end, wide):
        def add(x, acc):
            return acc + lax.dot_general(
                left(x),
                right(x),
                (((0,), (0,)), ((), ())),
                precision=HIGHEST,
                preferred_element_type=jnp.float32,
            )

        return lax.fori_loop(begin, end, add, jnp.zeros((128, wide), jnp.float32))

    def block(acc, at):
        total = acc[:OB, at : at + OB]
        for g in range(1, 4):
            total = total + acc[OB * g : OB * (g + 1), at + OB * g : at + OB * (g + 1)]
        return total

    def both(x):
        return jnp.concatenate([own(x), image(x)], axis=1)

    def add_up(n):
        source = part.at[0, 1 - core] if n == 0 else part.at[n, 0]
        copies = [
            pltpu.make_async_remote_copy(
                source,
                recv.at[slots[n] + k],
                rs.at[slots[n] + k],
                rr.at[slots[n] + k],
                device_id=peer,
                device_id_type=MESH,
            )
            for k, peer in enumerate(stages[n])
        ]
        for copy in copies:
            copy.start()
        for copy in copies:
            copy.wait()
        total = part[0, core] if n == 0 else part[n, 0]
        if n == 3:
            part[0, core] = total
            part[0, 1 - core] = recv[slots[3]]
            return
        for k in range(len(copies)):
            total = total + recv[slots[n] + k]
        part[n + 1, 0] = total

    def put(which, column, value):
        for half in range(2):
            part[0, half, which, :, OB * column : OB * (column + 1)] = value[
                half * (OB // 2) : (half + 1) * (OB // 2)
            ]

    part[...] = jnp.zeros_like(part)
    arrive(third)

    def step_three(x, carry):
        for j, value in enumerate(forward_stencil(e2, pot, x)):
            img[x, j] = value
        return carry

    lax.fori_loop(0, CX, step_three, 0)
    mine = gram(own, both, 0, CX, 256)

    @pl.when(band == 0)
    def _():
        put(0, 0, block(mine, 0))
        put(1, 0, block(mine, 128))
        across[0].wait_recv()
        crossed = gram(theirs, image, 0, CX // 2, 128)
        across[1].wait_recv()
        crossed = crossed + gram(theirs, image, CX // 2, CX, 128)
        put(1, 2, block(crossed, 0))

    @pl.when(band == 1)
    def _():
        put(0, 2, block(mine, 0))
        put(1, 3, block(mine, 128))
        across[0].wait_recv()
        crossed = gram(theirs, both, 0, CX // 2, 256)
        across[1].wait_recv()
        crossed = crossed + gram(theirs, both, CX // 2, CX, 256)
        put(0, 1, block(crossed, 0))
        put(1, 1, block(crossed, 128))

    for n in range(4):
        add_up(n)

    eye = (
        lax.broadcasted_iota(jnp.int32, (OB, OB), 0) == lax.broadcasted_iota(jnp.int32, (OB, OB), 1)
    ).astype(jnp.float32)

    def flip(m):
        return lax.dot_general(
            m,
            eye,
            (((0,), (0,)), ((), ())),
            precision=HIGHEST,
            preferred_element_type=jnp.float32,
        )

    def sums(which):
        rows = jnp.concatenate([part[0, 0, which], part[0, 1, which]], axis=0) * (1.0 / CELLS)
        return [rows[:, OB * k : OB * (k + 1)] for k in range(4)]

    def matrix(dst, a00, a01, a11):
        dst[0:OB, 0:OB] = a00
        dst[0:OB, OB : 2 * OB] = a01
        dst[OB : 2 * OB, OB : 2 * OB] = a11
        dst[OB : 2 * OB, 0:OB] = flip(a01)

    n_orb = 2 * OB
    row_id = lax.broadcasted_iota(jnp.int32, (n_orb, 128), 0)
    lane_id = lax.broadcasted_iota(jnp.int32, (n_orb, 128), 1)
    work[0] = (lane_id == row_id + n_orb).astype(jnp.float32)
    matrix(work.at[0], *sums(0)[:3])

    def eliminate(k, m):
        pivot_row = jnp.sum(jnp.where(row_id == k, m, 0.0), axis=0, keepdims=True)
        pivot_col = jnp.sum(jnp.where(lane_id == k, m, 0.0), axis=1, keepdims=True)
        pivot = jnp.sum(jnp.where(lane_id[:1] == k, pivot_row, 0.0), axis=1, keepdims=True)
        factor = jnp.where(row_id > k, pivot_col * (1.0 / pivot), 0.0)
        return m - factor * pivot_row

    m = lax.fori_loop(0, n_orb, eliminate, work[0])
    diag = jnp.sum(jnp.where(lane_id == row_id, m, 0.0), axis=1, keepdims=True)
    inverse = m * (1.0 / jnp.sqrt(diag))
    work[0] = inverse

    src = lax.broadcasted_iota(jnp.int32, (128, 128), 0)
    dst = lax.broadcasted_iota(jnp.int32, (128, 128), 1)
    same = src // OB == dst // OB
    mine_rows = work[0, pl.ds(pl.multiple_of(band * OB, OB), OB), :]

    def weights(column):
        pick = (src == n_orb + OB * column + lax.rem(dst, OB)).astype(jnp.float32)
        wide = jnp.dot(mine_rows, pick, precision=HIGHEST, preferred_element_type=jnp.float32)
        return jnp.where(same, jnp.concatenate([wide] * 4, axis=0), 0.0)

    coef[0] = weights(band)
    coef[1] = weights(0)

    def turn(x, carry):
        def times(rows, w):
            return lax.dot_general(
                rows,
                w,
                (((1,), (1,)), ((), ())),
                precision=HIGHEST,
                preferred_element_type=jnp.float32,
            )

        img[x] = times(own(x), coef[0]).reshape(NJ, CY, 128)

        @pl.when(band == 1)
        def _():
            img[x] = img[x] + times(theirs(x), coef[1]).reshape(NJ, CY, 128)

        return carry

    stores = []
    for half in range(2):
        lax.fori_loop(half * CX // 2, (half + 1) * CX // 2, turn, 0)
        for j in range(NJ):
            stores.append(
                pltpu.make_async_copy(
                    img.at[parts[half], j],
                    out_ref.at[0, 0, parts[half], :, pl.ds(128 * j, 128)],
                    out_sem.at[half, j],
                )
            )
            stores[-1].start()

    s00, s01, s10, s11 = sums(1)
    matrix(work.at[1], s00 + flip(s00), s01 + flip(s10), s11 + flip(s11))
    pick = (
        lax.broadcasted_iota(jnp.int32, (128, n_orb), 0)
        == n_orb + lax.broadcasted_iota(jnp.int32, (128, n_orb), 1)
    ).astype(jnp.float32)
    inv = jnp.dot(work[0], pick, precision=HIGHEST, preferred_element_type=jnp.float32)
    left = jnp.dot(
        inv, work[1, :, 0:n_orb], precision=HIGHEST, preferred_element_type=jnp.float32
    )
    proj_ref[...] = lax.dot_general(
        left,
        inv,
        (((1,), (1,)), ((), ())),
        precision=HIGHEST,
        preferred_element_type=jnp.float32,
    )
    for copy in stores:
        copy.wait()
    drain(first)
    drain(second)
    drain(third)
    for copy in across:
        copy.wait_send()


def local(orbitals, potential):
    big = (XO * 2 + CX, JO * 2 + NJ, YO * 2 + CY, 128)
    tile = (CX, NJ, CY, 128)
    vmem = pl.BlockSpec(memory_space=pltpu.VMEM)
    hbm = pl.BlockSpec(memory_space=pl.ANY)
    f32 = jnp.float32
    dma = pltpu.SemaphoreType.DMA
    return pl.pallas_call(
        filter_kernel,
        out_shape=(
            jax.ShapeDtypeStruct((1, 1, CX, CY, CZ * OB), f32),
            jax.ShapeDtypeStruct((2 * OB, 2 * OB), f32),
        ),
        in_specs=[hbm, hbm],
        out_specs=(hbm, vmem),
        scratch_shapes=[
            pltpu.VMEM(big, f32),
            pltpu.VMEM(big, f32),
            pltpu.VMEM(big, f32),
            pltpu.VMEM(tile, f32),
            pltpu.VMEM(tile, f32),
            pltpu.VMEM(tile, f32),
            pltpu.VMEM((4, 2, 2, OB // 2, 128), f32),
            pltpu.VMEM((24, 2, OB // 2, 128), f32),
            pltpu.VMEM((2, 2 * OB, 128), f32),
            pltpu.VMEM((2, 128, 128), f32),
            pltpu.VMEM((1, CX, CY, CZ), f32),
            dma((NJ + 1,)),
            dma((2, NJ)),
            dma((3, 6)),
            dma((3, 6)),
            dma((2,)),
            dma((2,)),
            dma((24,)),
            dma((24,)),
        ],
        compiler_params=pltpu.CompilerParams(
            collective_id=0, has_side_effects=True, vmem_limit_bytes=60 << 20
        ),
    )(orbitals, potential)


def solution(mesh):
    return jax.shard_map(
        local,
        mesh=mesh,
        in_specs=(P("dom", "band", None, None, None), P("dom", None, None, None)),
        out_specs=(P("dom", "band", None, None, None), P()),
        check_vma=False,
    )
```

```python
import functools

import jax
import jax.numpy as jnp
from jax import lax
from jax.experimental import pallas as pl
from jax.experimental.pallas import tpu as pltpu
from jax.sharding import PartitionSpec as P

COEFFS = (
    -5369.0 / 1800.0,
    12.0 / 7.0,
    -15.0 / 56.0,
    10.0 / 189.0,
    -1.0 / 112.0,
    2.0 / 1925.0,
    -1.0 / 16632.0,
)
SPACING = 0.32
CENTER = 71.0
HALFWIDTH = 69.0
KINETIC = -0.5 / SPACING**2 / HALFWIDTH
A = tuple(KINETIC * c for c in COEFFS)

CX, CY, CZ, OB = 12, 32, 32, 32
PX, PY, PZ = 8, 4, 4
NJ = CZ * OB // 128
CELLS = PX * CX * PY * CY * PZ * CZ
MESH = pl.DeviceIdType.MESH
HIGHEST = lax.Precision.HIGHEST
XO, JO, YO = 6, 2, 8
OWN = (pl.ds(XO, CX), pl.ds(JO, NJ), pl.ds(YO, CY))


def stencil(field, pot, x):
    lane = lax.broadcasted_iota(jnp.int32, (CY, 128), 1)

    def tile(j, dx=0, dy=0):
        return field[XO + x + dx, JO + j, pl.ds(YO + dy, CY), :]

    def partial(j):
        m2, m1, v, p1 = tile(j - 2), tile(j - 1), tile(j), tile(j + 1)
        t1 = A[3] * m1 + A[1] * v + A[5] * p1
        t2 = A[2] * (v + m1) + A[6] * (p1 + m2)
        t3 = A[3] * v + A[1] * m1 + A[5] * m2
        return (
            pltpu.roll(t1, 96, 1),
            pltpu.roll(t2, 64, 1),
            pltpu.roll(t3, 32, 1),
        )

    out = []
    low = partial(0)
    for j in range(NJ):
        high = partial(j + 1)
        acc = jnp.where(lane < 96, low[0], high[0])
        acc = acc + jnp.where(lane < 64, low[1], high[1])
        acc = acc + jnp.where(lane < 32, low[2], high[2])
        low = high
        acc = acc + pot[x, j] * tile(j)
        for k in range(1, 7):
            terms = tile(j, k) + tile(j, -k) + tile(j, 0, k) + tile(j, 0, -k)
            if k == 4:
                terms = terms + (tile(j + 1) + tile(j - 1))
            acc = acc + A[k] * terms
        out.append(acc)
    return out


def backward_stencil(field, pot, x):
    lane = lax.broadcasted_iota(jnp.int32, (CY, 128), 1)

    def tile(j, dx=0, dy=0):
        return field[XO + x + dx, JO + j, pl.ds(YO + dy, CY), :]

    def partial(j):
        m1, m2 = tile(j - 1), tile(j - 2)
        return (
            pltpu.roll(A[3] * m1, 96, 1),
            pltpu.roll(A[2] * m1 + A[6] * m2, 64, 1),
            pltpu.roll(A[1] * m1 + A[5] * m2, 32, 1),
        )

    out = []
    low = partial(0)
    for j in range(NJ):
        high = partial(j + 1)
        acc = jnp.where(lane < 96, low[0], high[0])
        acc = acc + jnp.where(lane < 64, low[1], high[1])
        acc = acc + jnp.where(lane < 32, low[2], high[2])
        low = high
        acc = acc + 0.5 * pot[x, j] * tile(j)
        for k in range(1, 7):
            terms = tile(j, -k) + tile(j, 0, -k)
            if k == 4:
                terms = terms + tile(j - 1)
            acc = acc + A[k] * terms
        out.append(acc)
    return out


def filter_kernel(
    orb_ref,
    pot_hbm,
    out_ref,
    proj_ref,
    e0,
    e1,
    e2,
    img,
    pot,
    other,
    part,
    gathered,
    halved,
    piece,
    summed,
    recv,
    work,
    coef,
    pot_ref,
    load_sem,
    out_sem,
    hs,
    hr,
    bs,
    br,
    rs,
    rr,
):
    dom = lax.axis_index("dom")
    band = lax.axis_index("band")
    tz = lax.rem(dom, PZ)
    ty = lax.rem(dom // PZ, PY)
    tx = dom // (PY * PZ)
    px, py, pz, core = dom // 32, lax.rem(dom // 8, 4), lax.rem(dom // 2, 4), lax.rem(dom, 2)

    loads = [
        pltpu.make_async_copy(
            orb_ref.at[0, 0, :, :, pl.ds(128 * j, 128)],
            e0.at[pl.ds(XO, CX), JO + j, pl.ds(YO, CY)],
            load_sem.at[j],
        )
        for j in range(NJ)
    ]
    loads.append(pltpu.make_async_copy(pot_hbm, pot_ref, load_sem.at[NJ]))
    for copy in loads:
        copy.start()

    def place(x, y, z, c):
        return ((x * 4 + y) * 4 + z) * 2 + c

    faces = (
        (PY * PZ, tx, PX),
        (PZ, ty, PY),
        (1, tz, PZ),
    )
    twin = (place(px, py, pz, 1 - core), band)
    column = [
        (place(px, py, lax.rem(pz + k, 4), core), lax.rem(band + b, 2))
        for k in range(4)
        for b in range(2)
        if k or b
    ]
    plane = [
        (place(lax.rem(px + i, 4), lax.rem(py + k, 4), pz, core), band)
        for i in range(4)
        for k in range(4)
        if i or k
    ]

    barrier = pltpu.get_barrier_semaphore()
    count = jnp.int32(23)
    for peer in [twin] + column + plane:
        pl.semaphore_signal(barrier, inc=1, device_id=peer, device_id_type=MESH)
    for stride, at, n in faces:
        has_low, has_high = at > 0, at < n - 1
        count = count + has_low.astype(jnp.int32) + has_high.astype(jnp.int32)

        @pl.when(has_low)
        def _():
            pl.semaphore_signal(barrier, inc=1, device_id=(dom - stride, band), device_id_type=MESH)

        @pl.when(has_high)
        def _():
            pl.semaphore_signal(barrier, inc=1, device_id=(dom + stride, band), device_id_type=MESH)

    row = lax.broadcasted_iota(jnp.int32, (CZ, CZ * OB), 0)
    col = lax.broadcasted_iota(jnp.int32, (CZ, CZ * OB), 1)
    spread = (row == col // OB).astype(jnp.float32)

    def spread_pot(x, carry):
        scaled = (pot_ref[0, x] - CENTER) * (1.0 / HALFWIDTH) + 3.0 * A[0]
        wide = jnp.dot(scaled, spread, precision=HIGHEST, preferred_element_type=jnp.float32)
        for j in range(NJ):
            pot[x, j] = wide[:, 128 * j : 128 * (j + 1)]
        return carry

    pl.semaphore_wait(barrier, count)

    def sections(dim):
        sizes = ((XO, CX, 6), (JO, NJ, 2), (YO, CY, 6))
        axis = (0, 2, 1)[dim]
        start, extent, depth = sizes[axis]
        picks = []
        for at in (start, start + extent - depth, start - depth, start + extent):
            index = list(OWN)
            index[axis] = pl.ds(at, depth)
            picks.append(tuple(index))
        return picks

    def halo(field, step):
        copies = []
        for dim, (stride, at, n) in enumerate(faces):
            low_rim, high_rim, below, above = sections(dim)
            up = pltpu.make_async_remote_copy(
                field.at[high_rim],
                field.at[below],
                hs.at[step, 2 * dim],
                hr.at[step, 2 * dim],
                device_id=(lax.rem(dom + stride, 128), band),
                device_id_type=MESH,
            )
            down = pltpu.make_async_remote_copy(
                field.at[low_rim],
                field.at[above],
                hs.at[step, 2 * dim + 1],
                hr.at[step, 2 * dim + 1],
                device_id=(lax.rem(dom - stride + 128, 128), band),
                device_id_type=MESH,
            )
            copies.append((up, at < n - 1, at > 0, below))
            copies.append((down, at > 0, at < n - 1, above))
        return copies

    def start(copies, field):
        for copy, sends, receives, landing in copies:

            @pl.when(sends)
            def _():
                copy.start()

        for copy, sends, receives, landing in copies:

            @pl.when(jnp.logical_not(receives))
            def _():
                xs, js, ys = landing

                def clear(i, carry):
                    field[xs.start + i, js, ys] = jnp.zeros((js.size, ys.size, 128), jnp.float32)
                    return carry

                lax.fori_loop(0, xs.size, clear, 0)

    def arrive(copies):
        for copy, sends, receives, landing in copies:

            @pl.when(receives)
            def _():
                copy.wait_recv()

    def drain(copies):
        for copy, sends, receives, landing in copies:

            @pl.when(sends)
            def _():
                copy.wait_send()

    for copy in loads:
        copy.wait()
    first = halo(e0, 0)
    start(first, e0)
    lax.fori_loop(0, CX, spread_pot, 0)
    arrive(first)

    def step_one(x, carry):
        for j, value in enumerate(stencil(e0, pot, x)):
            e1[XO + x, JO + j, pl.ds(YO, CY), :] = value
        return carry

    lax.fori_loop(0, CX, step_one, 0)
    second = halo(e1, 1)
    start(second, e1)
    arrive(second)

    def step_two(x, carry):
        for j, value in enumerate(stencil(e1, pot, x)):
            own = e0[XO + x, JO + j, pl.ds(YO, CY), :]
            e2[XO + x, JO + j, pl.ds(YO, CY), :] = 2.0 * value - own
        return carry

    lax.fori_loop(0, CX, step_two, 0)
    third = halo(e2, 2)[0::2]
    start(third, e2)
    partner = (dom, 1 - band)
    parts = (pl.ds(0, CX // 2), pl.ds(CX // 2, CX // 2))
    across = [
        pltpu.make_async_remote_copy(
            e2.at[pl.ds(XO + planes.start, planes.size), OWN[1], OWN[2]],
            other.at[planes],
            bs.at[at],
            br.at[at],
            device_id=partner,
            device_id_type=MESH,
        )
        for at, planes in enumerate(parts)
    ]
    for copy in across:
        copy.start()

    def own(x):
        return e2[XO + x, pl.ds(JO, NJ), pl.ds(YO, CY), :].reshape(NJ * CY, 128)

    def theirs(x):
        return other[x].reshape(NJ * CY, 128)

    def image(x):
        return img[x].reshape(NJ * CY, 128)

    def gram(left, right, begin, end, wide):
        def add(x, acc):
            return acc + lax.dot_general(
                left(x),
                right(x),
                (((0,), (0,)), ((), ())),
                precision=HIGHEST,
                preferred_element_type=jnp.float32,
            )

        return lax.fori_loop(begin, end, add, jnp.zeros((128, wide), jnp.float32))

    def block(acc, at):
        total = acc[:OB, at : at + OB]
        for g in range(1, 4):
            total = total + acc[OB * g : OB * (g + 1), at + OB * g : at + OB * (g + 1)]
        return total

    def both(x):
        return jnp.concatenate([own(x), image(x)], axis=1)

    def swap(copies):
        for copy in copies:
            copy.start()
        for copy in copies:
            copy.wait()

    def message(source, dest, slot, peer):
        return pltpu.make_async_remote_copy(
            source, dest, rs.at[slot], rr.at[slot], device_id=peer, device_id_type=MESH
        )

    def add_up():
        swap([message(part.at[1 - core], gathered, 0, twin)])
        halved[...] = part[core] + gathered[...]
        swap(
            [
                message(halved.at[lax.rem(pz + (k + 1) // 2, 4)], recv.at[k], 1 + k, peer)
                for k, peer in enumerate(column)
            ]
        )
        total = halved[pz]
        for k in range(len(column)):
            total = total + recv[k]
        piece[0] = total
        swap(
            [
                message(piece.at[0], recv.at[7 + k], 8 + k, peer)
                for k, peer in enumerate(plane)
            ]
        )
        for k in range(len(plane)):
            total = total + recv[7 + k]
        summed[core, pz] = total
        swap(
            [
                message(summed.at[core, pz], summed.at[core, pz], 22 + k, column[2 * k - 1])
                for k in range(1, 4)
            ]
        )
        swap([message(summed.at[core], summed.at[core], 26, twin)])

    def put(which, column, value):
        for half in range(2):
            for t in range(2):
                at = half * (OB // 2) + 8 * t
                part[half, 2 * which + t, :, OB * column : OB * (column + 1)] = value[at : at + 8]

    part[...] = jnp.zeros_like(part)
    arrive(third)

    def step_three(x, carry):
        for j, value in enumerate(backward_stencil(e2, pot, x)):
            img[x, j] = value
        return carry

    lax.fori_loop(0, CX, step_three, 0)
    mine = gram(own, both, 0, CX, 256)

    @pl.when(band == 0)
    def _():
        put(0, 0, block(mine, 0))
        put(1, 0, block(mine, 128))
        across[0].wait_recv()
        crossed = gram(theirs, image, 0, CX // 2, 128)
        across[1].wait_recv()
        crossed = crossed + gram(theirs, image, CX // 2, CX, 128)
        put(1, 2, block(crossed, 0))

    @pl.when(band == 1)
    def _():
        put(0, 2, block(mine, 0))
        put(1, 3, block(mine, 128))
        across[0].wait_recv()
        crossed = gram(theirs, both, 0, CX // 2, 256)
        across[1].wait_recv()
        crossed = crossed + gram(theirs, both, CX // 2, CX, 256)
        put(0, 1, block(crossed, 0))
        put(1, 1, block(crossed, 128))

    add_up()

    eye = (
        lax.broadcasted_iota(jnp.int32, (OB, OB), 0) == lax.broadcasted_iota(jnp.int32, (OB, OB), 1)
    ).astype(jnp.float32)

    def flip(m):
        return lax.dot_general(
            m,
            eye,
            (((0,), (0,)), ((), ())),
            precision=HIGHEST,
            preferred_element_type=jnp.float32,
        )

    def sums(which):
        pieces = [summed[half, 2 * which + t] for half in range(2) for t in range(2)]
        rows = jnp.concatenate(pieces, axis=0) * (1.0 / CELLS)
        return [rows[:, OB * k : OB * (k + 1)] for k in range(4)]

    def matrix(dst, a00, a01, a11):
        dst[0:OB, 0:OB] = a00
        dst[0:OB, OB : 2 * OB] = a01
        dst[OB : 2 * OB, OB : 2 * OB] = a11
        dst[OB : 2 * OB, 0:OB] = flip(a01)

    n_orb = 2 * OB
    row_id = lax.broadcasted_iota(jnp.int32, (n_orb, 128), 0)
    lane_id = lax.broadcasted_iota(jnp.int32, (n_orb, 128), 1)
    work[0] = (lane_id == row_id + n_orb).astype(jnp.float32)
    matrix(work.at[0], *sums(0)[:3])

    def eliminate(step, m):
        k = 2 * step
        row0 = jnp.sum(jnp.where(row_id == k, m, 0.0), axis=0, keepdims=True)
        row1 = jnp.sum(jnp.where(row_id == k + 1, m, 0.0), axis=0, keepdims=True)
        col0 = jnp.sum(jnp.where(lane_id == k, m, 0.0), axis=1, keepdims=True)
        col1 = jnp.sum(jnp.where(lane_id == k + 1, m, 0.0), axis=1, keepdims=True)

        def entry(row, at):
            return jnp.sum(jnp.where(lane_id[:1] == at, row, 0.0), axis=1, keepdims=True)

        inv0 = 1.0 / entry(row0, k)
        ratio0 = entry(row1, k) * inv0
        across0 = entry(row0, k + 1)
        row1 = row1 - ratio0 * row0
        pivot1 = entry(row1, k + 1)
        col1 = col1 - (across0 * inv0) * col0
        factor0 = jnp.where(row_id > k, col0 * inv0, 0.0)
        factor1 = jnp.where(row_id > k + 1, col1 * (1.0 / pivot1), 0.0)
        return m - factor0 * row0 - factor1 * row1

    m = lax.fori_loop(0, n_orb // 2, eliminate, work[0])
    diag = jnp.sum(jnp.where(lane_id == row_id, m, 0.0), axis=1, keepdims=True)
    inverse = m * (1.0 / jnp.sqrt(diag))
    work[0] = inverse

    src = lax.broadcasted_iota(jnp.int32, (128, 128), 0)
    dst = lax.broadcasted_iota(jnp.int32, (128, 128), 1)
    same = src // OB == dst // OB
    mine_rows = work[0, pl.ds(pl.multiple_of(band * OB, OB), OB), :]

    def weights(column):
        pick = (src == n_orb + OB * column + lax.rem(dst, OB)).astype(jnp.float32)
        wide = jnp.dot(mine_rows, pick, precision=HIGHEST, preferred_element_type=jnp.float32)
        return jnp.where(same, jnp.concatenate([wide] * 4, axis=0), 0.0)

    coef[0] = weights(band)
    coef[1] = weights(0)

    def turn(x, carry):
        def times(rows, w):
            return lax.dot_general(
                rows,
                w,
                (((1,), (1,)), ((), ())),
                precision=HIGHEST,
                preferred_element_type=jnp.float32,
            )

        img[x] = times(own(x), coef[0]).reshape(NJ, CY, 128)

        @pl.when(band == 1)
        def _():
            img[x] = img[x] + times(theirs(x), coef[1]).reshape(NJ, CY, 128)

        return carry

    stores = []
    for half in range(2):
        lax.fori_loop(half * CX // 2, (half + 1) * CX // 2, turn, 0)
        for j in range(NJ):
            stores.append(
                pltpu.make_async_copy(
                    img.at[parts[half], j],
                    out_ref.at[0, 0, parts[half], :, pl.ds(128 * j, 128)],
                    out_sem.at[half, j],
                )
            )
            stores[-1].start()

    s00, s01, s10, s11 = sums(1)
    matrix(work.at[1], s00 + flip(s00), s01 + flip(s10), s11 + flip(s11))
    pick = (
        lax.broadcasted_iota(jnp.int32, (128, n_orb), 0)
        == n_orb + lax.broadcasted_iota(jnp.int32, (128, n_orb), 1)
    ).astype(jnp.float32)
    inv = jnp.dot(work[0], pick, precision=HIGHEST, preferred_element_type=jnp.float32)
    left = jnp.dot(
        inv, work[1, :, 0:n_orb], precision=HIGHEST, preferred_element_type=jnp.float32
    )
    proj_ref[...] = lax.dot_general(
        left,
        inv,
        (((1,), (1,)), ((), ())),
        precision=HIGHEST,
        preferred_element_type=jnp.float32,
    )
    for copy in stores:
        copy.wait()
    drain(first)
    drain(second)
    drain(third)
    for copy in across:
        copy.wait_send()


def local(orbitals, potential):
    big = (XO * 2 + CX, JO * 2 + NJ, YO * 2 + CY, 128)
    tile = (CX, NJ, CY, 128)
    vmem = pl.BlockSpec(memory_space=pltpu.VMEM)
    hbm = pl.BlockSpec(memory_space=pl.ANY)
    f32 = jnp.float32
    dma = pltpu.SemaphoreType.DMA
    return pl.pallas_call(
        filter_kernel,
        out_shape=(
            jax.ShapeDtypeStruct((1, 1, CX, CY, CZ * OB), f32),
            jax.ShapeDtypeStruct((2 * OB, 2 * OB), f32),
        ),
        in_specs=[hbm, hbm],
        out_specs=(hbm, vmem),
        scratch_shapes=[
            pltpu.VMEM(big, f32),
            pltpu.VMEM(big, f32),
            pltpu.VMEM(big, f32),
            pltpu.VMEM(tile, f32),
            pltpu.VMEM(tile, f32),
            pltpu.VMEM(tile, f32),
            pltpu.VMEM((2, 4, 8, 128), f32),
            pltpu.VMEM((4, 8, 128), f32),
            pltpu.VMEM((4, 8, 128), f32),
            pltpu.VMEM((1, 8, 128), f32),
            pltpu.VMEM((2, 4, 8, 128), f32),
            pltpu.VMEM((22, 8, 128), f32),
            pltpu.VMEM((2, 2 * OB, 128), f32),
            pltpu.VMEM((2, 128, 128), f32),
            pltpu.VMEM((1, CX, CY, CZ), f32),
            dma((NJ + 1,)),
            dma((2, NJ)),
            dma((3, 6)),
            dma((3, 6)),
            dma((2,)),
            dma((2,)),
            dma((27,)),
            dma((27,)),
        ],
        compiler_params=pltpu.CompilerParams(
            collective_id=0, has_side_effects=True, vmem_limit_bytes=60 << 20
        ),
    )(orbitals, potential)


def solution(mesh):
    return jax.shard_map(
        local,
        mesh=mesh,
        in_specs=(P("dom", "band", None, None, None), P("dom", None, None, None)),
        out_specs=(P("dom", "band", None, None, None), P()),
        check_vma=False,
    )
```

```python
import functools

import jax
import jax.numpy as jnp
from jax import lax
from jax.experimental import pallas as pl
from jax.experimental.pallas import tpu as pltpu
from jax.sharding import PartitionSpec as P

COEFFS = (
    -5369.0 / 1800.0,
    12.0 / 7.0,
    -15.0 / 56.0,
    10.0 / 189.0,
    -1.0 / 112.0,
    2.0 / 1925.0,
    -1.0 / 16632.0,
)
SPACING = 0.32
CENTER = 71.0
HALFWIDTH = 69.0
KINETIC = -0.5 / SPACING**2 / HALFWIDTH
A = tuple(KINETIC * c for c in COEFFS)

CX, CY, CZ, OB = 12, 32, 32, 32
PX, PY, PZ = 8, 4, 4
NJ = CZ * OB // 128
CELLS = PX * CX * PY * CY * PZ * CZ
MESH = pl.DeviceIdType.MESH
HIGHEST = lax.Precision.HIGHEST
XO, JO, YO = 6, 2, 8
OWN = (pl.ds(XO, CX), pl.ds(JO, NJ), pl.ds(YO, CY))


def stencil(field, pot, x):
    lane = lax.broadcasted_iota(jnp.int32, (CY, 128), 1)

    def tile(j, dx=0, dy=0):
        return field[XO + x + dx, JO + j, pl.ds(YO + dy, CY), :]

    def partial(j):
        m2, m1, v, p1 = tile(j - 2), tile(j - 1), tile(j), tile(j + 1)
        t1 = A[3] * m1 + A[1] * v + A[5] * p1
        t2 = A[2] * (v + m1) + A[6] * (p1 + m2)
        t3 = A[3] * v + A[1] * m1 + A[5] * m2
        return (
            pltpu.roll(t1, 96, 1),
            pltpu.roll(t2, 64, 1),
            pltpu.roll(t3, 32, 1),
        )

    out = []
    low = partial(0)
    for j in range(NJ):
        high = partial(j + 1)
        acc = jnp.where(lane < 96, low[0], high[0])
        acc = acc + jnp.where(lane < 64, low[1], high[1])
        acc = acc + jnp.where(lane < 32, low[2], high[2])
        low = high
        acc = acc + pot[x, j] * tile(j)
        for k in range(1, 7):
            terms = tile(j, k) + tile(j, -k) + tile(j, 0, k) + tile(j, 0, -k)
            if k == 4:
                terms = terms + (tile(j + 1) + tile(j - 1))
            acc = acc + A[k] * terms
        out.append(acc)
    return out


def backward_stencil(field, pot, x):
    lane = lax.broadcasted_iota(jnp.int32, (CY, 128), 1)

    def tile(j, dx=0, dy=0):
        return field[XO + x + dx, JO + j, pl.ds(YO + dy, CY), :]

    def partial(j):
        m1, m2 = tile(j - 1), tile(j - 2)
        return (
            pltpu.roll(A[3] * m1, 96, 1),
            pltpu.roll(A[2] * m1 + A[6] * m2, 64, 1),
            pltpu.roll(A[1] * m1 + A[5] * m2, 32, 1),
        )

    out = []
    low = partial(0)
    for j in range(NJ):
        high = partial(j + 1)
        acc = jnp.where(lane < 96, low[0], high[0])
        acc = acc + jnp.where(lane < 64, low[1], high[1])
        acc = acc + jnp.where(lane < 32, low[2], high[2])
        low = high
        acc = acc + 0.5 * pot[x, j] * tile(j)
        for k in range(1, 7):
            terms = tile(j, -k) + tile(j, 0, -k)
            if k == 4:
                terms = terms + tile(j - 1)
            acc = acc + A[k] * terms
        out.append(acc)
    return out


def filter_kernel(
    orb_ref,
    pot_hbm,
    out_ref,
    proj_ref,
    e0,
    e1,
    e2,
    img,
    pot,
    other,
    part,
    gathered,
    halved,
    piece,
    summed,
    recv,
    work,
    coef,
    pot_ref,
    load_sem,
    out_sem,
    hs,
    hr,
    bs,
    br,
    rs,
    rr,
):
    dom = lax.axis_index("dom")
    band = lax.axis_index("band")
    tz = lax.rem(dom, PZ)
    ty = lax.rem(dom // PZ, PY)
    tx = dom // (PY * PZ)
    px, py, pz, core = dom // 32, lax.rem(dom // 8, 4), lax.rem(dom // 2, 4), lax.rem(dom, 2)

    loads = [
        pltpu.make_async_copy(
            orb_ref.at[0, 0, :, :, pl.ds(128 * j, 128)],
            e0.at[pl.ds(XO, CX), JO + j, pl.ds(YO, CY)],
            load_sem.at[j],
        )
        for j in range(NJ)
    ]
    loads.append(pltpu.make_async_copy(pot_hbm, pot_ref, load_sem.at[NJ]))
    for copy in loads:
        copy.start()

    def place(x, y, z, c):
        return ((x * 4 + y) * 4 + z) * 2 + c

    faces = (
        (PY * PZ, tx, PX),
        (PZ, ty, PY),
        (1, tz, PZ),
    )
    twin = (place(px, py, pz, 1 - core), band)
    column = [
        (place(px, py, lax.rem(pz + k, 4), core), lax.rem(band + b, 2))
        for k in range(4)
        for b in range(2)
        if k or b
    ]
    plane = [
        (place(lax.rem(px + i, 4), lax.rem(py + k, 4), pz, core), band)
        for i in range(4)
        for k in range(4)
        if i or k
    ]

    barrier = pltpu.get_barrier_semaphore()
    count = jnp.int32(23)
    for peer in [twin] + column + plane:
        pl.semaphore_signal(barrier, inc=1, device_id=peer, device_id_type=MESH)
    for stride, at, n in faces:
        has_low, has_high = at > 0, at < n - 1
        count = count + has_low.astype(jnp.int32) + has_high.astype(jnp.int32)

        @pl.when(has_low)
        def _():
            pl.semaphore_signal(barrier, inc=1, device_id=(dom - stride, band), device_id_type=MESH)

        @pl.when(has_high)
        def _():
            pl.semaphore_signal(barrier, inc=1, device_id=(dom + stride, band), device_id_type=MESH)

    row = lax.broadcasted_iota(jnp.int32, (CZ, CZ * OB), 0)
    col = lax.broadcasted_iota(jnp.int32, (CZ, CZ * OB), 1)
    spread = (row == col // OB).astype(jnp.float32)

    def spread_pot(x, carry):
        scaled = (pot_ref[0, x] - CENTER) * (1.0 / HALFWIDTH) + 3.0 * A[0]
        wide = jnp.dot(scaled, spread, precision=HIGHEST, preferred_element_type=jnp.float32)
        for j in range(NJ):
            pot[x, j] = wide[:, 128 * j : 128 * (j + 1)]
        return carry

    pl.semaphore_wait(barrier, count)

    def sections(dim):
        sizes = ((XO, CX, 6), (JO, NJ, 2), (YO, CY, 6))
        axis = (0, 2, 1)[dim]
        start, extent, depth = sizes[axis]
        picks = []
        for at in (start, start + extent - depth, start - depth, start + extent):
            index = list(OWN)
            index[axis] = pl.ds(at, depth)
            picks.append(tuple(index))
        return picks

    def halo(field, step):
        copies = []
        for dim, (stride, at, n) in enumerate(faces):
            low_rim, high_rim, below, above = sections(dim)
            up = pltpu.make_async_remote_copy(
                field.at[high_rim],
                field.at[below],
                hs.at[step, 2 * dim],
                hr.at[step, 2 * dim],
                device_id=(lax.rem(dom + stride, 128), band),
                device_id_type=MESH,
            )
            down = pltpu.make_async_remote_copy(
                field.at[low_rim],
                field.at[above],
                hs.at[step, 2 * dim + 1],
                hr.at[step, 2 * dim + 1],
                device_id=(lax.rem(dom - stride + 128, 128), band),
                device_id_type=MESH,
            )
            copies.append((up, at < n - 1, at > 0, below))
            copies.append((down, at > 0, at < n - 1, above))
        return [copies[i] for i in (4, 5, 2, 3, 0, 1)]

    def start(copies, field):
        for copy, sends, receives, landing in copies:

            @pl.when(sends)
            def _():
                copy.start()

        for copy, sends, receives, landing in copies:

            @pl.when(jnp.logical_not(receives))
            def _():
                xs, js, ys = landing

                def clear(i, carry):
                    field[xs.start + i, js, ys] = jnp.zeros((js.size, ys.size, 128), jnp.float32)
                    return carry

                lax.fori_loop(0, xs.size, clear, 0)

    def arrive(copies):
        for copy, sends, receives, landing in copies:

            @pl.when(receives)
            def _():
                copy.wait_recv()

    def drain(copies):
        for copy, sends, receives, landing in copies:

            @pl.when(sends)
            def _():
                copy.wait_send()

    for copy in loads:
        copy.wait()
    first = halo(e0, 0)
    start(first, e0)
    lax.fori_loop(0, CX, spread_pot, 0)
    arrive(first)

    def step_one(x, carry):
        for j, value in enumerate(stencil(e0, pot, x)):
            e1[XO + x, JO + j, pl.ds(YO, CY), :] = value
        return carry

    lax.fori_loop(0, CX, step_one, 0)
    second = halo(e1, 1)
    start(second, e1)
    arrive(second)

    def step_two(x, carry):
        for j, value in enumerate(stencil(e1, pot, x)):
            own = e0[XO + x, JO + j, pl.ds(YO, CY), :]
            e2[XO + x, JO + j, pl.ds(YO, CY), :] = 2.0 * value - own
        return carry

    lax.fori_loop(0, CX, step_two, 0)
    third = halo(e2, 2)[0::2]
    start(third, e2)
    partner = (dom, 1 - band)
    parts = (pl.ds(0, CX // 2), pl.ds(CX // 2, CX // 2))
    across = [
        pltpu.make_async_remote_copy(
            e2.at[pl.ds(XO + planes.start, planes.size), OWN[1], OWN[2]],
            other.at[planes],
            bs.at[at],
            br.at[at],
            device_id=partner,
            device_id_type=MESH,
        )
        for at, planes in enumerate(parts)
    ]
    for copy in across:
        copy.start()

    def own(x):
        return e2[XO + x, pl.ds(JO, NJ), pl.ds(YO, CY), :].reshape(NJ * CY, 128)

    def theirs(x):
        return other[x].reshape(NJ * CY, 128)

    def image(x):
        return img[x].reshape(NJ * CY, 128)

    def gram(left, right, begin, end, wide):
        def add(x, acc):
            return acc + lax.dot_general(
                left(x),
                right(x),
                (((0,), (0,)), ((), ())),
                precision=HIGHEST,
                preferred_element_type=jnp.float32,
            )

        return lax.fori_loop(begin, end, add, jnp.zeros((128, wide), jnp.float32))

    def block(acc, at):
        total = acc[:OB, at : at + OB]
        for g in range(1, 4):
            total = total + acc[OB * g : OB * (g + 1), at + OB * g : at + OB * (g + 1)]
        return total

    def both(x):
        return jnp.concatenate([own(x), image(x)], axis=1)

    def swap(copies):
        for copy in copies:
            copy.start()
        for copy in copies:
            copy.wait()

    def message(source, dest, slot, peer):
        return pltpu.make_async_remote_copy(
            source, dest, rs.at[slot], rr.at[slot], device_id=peer, device_id_type=MESH
        )

    def add_up():
        swap([message(part.at[1 - core], gathered, 0, twin)])
        halved[...] = part[core] + gathered[...]
        swap(
            [
                message(halved.at[lax.rem(pz + (k + 1) // 2, 4)], recv.at[k], 1 + k, peer)
                for k, peer in enumerate(column)
            ]
        )
        total = halved[pz]
        for k in range(len(column)):
            total = total + recv[k]
        piece[0] = total
        swap(
            [
                message(piece.at[0], recv.at[7 + k], 8 + k, peer)
                for k, peer in enumerate(plane)
            ]
        )
        for k in range(len(plane)):
            total = total + recv[7 + k]
        summed[core, pz] = total
        swap(
            [
                message(summed.at[core, pz], summed.at[core, pz], 22 + k, column[2 * k - 1])
                for k in range(1, 4)
            ]
        )
        swap([message(summed.at[core], summed.at[core], 26, twin)])

    def put(which, column, value):
        for half in range(2):
            for t in range(2):
                at = half * (OB // 2) + 8 * t
                part[half, 2 * which + t, :, OB * column : OB * (column + 1)] = value[at : at + 8]

    part[...] = jnp.zeros_like(part)
    arrive(third)

    def step_three(x, carry):
        for j, value in enumerate(backward_stencil(e2, pot, x)):
            img[x, j] = value
        return carry

    lax.fori_loop(0, CX, step_three, 0)
    mine = gram(own, both, 0, CX, 256)

    @pl.when(band == 0)
    def _():
        put(0, 0, block(mine, 0))
        put(1, 0, block(mine, 128))
        across[0].wait_recv()
        crossed = gram(theirs, image, 0, CX // 2, 128)
        across[1].wait_recv()
        crossed = crossed + gram(theirs, image, CX // 2, CX, 128)
        put(1, 2, block(crossed, 0))

    @pl.when(band == 1)
    def _():
        put(0, 2, block(mine, 0))
        put(1, 3, block(mine, 128))
        across[0].wait_recv()
        crossed = gram(theirs, both, 0, CX // 2, 256)
        across[1].wait_recv()
        crossed = crossed + gram(theirs, both, CX // 2, CX, 256)
        put(0, 1, block(crossed, 0))
        put(1, 1, block(crossed, 128))

    add_up()

    eye = (
        lax.broadcasted_iota(jnp.int32, (OB, OB), 0) == lax.broadcasted_iota(jnp.int32, (OB, OB), 1)
    ).astype(jnp.float32)

    def flip(m):
        return lax.dot_general(
            m,
            eye,
            (((0,), (0,)), ((), ())),
            precision=HIGHEST,
            preferred_element_type=jnp.float32,
        )

    def sums(which):
        pieces = [summed[half, 2 * which + t] for half in range(2) for t in range(2)]
        rows = jnp.concatenate(pieces, axis=0) * (1.0 / CELLS)
        return [rows[:, OB * k : OB * (k + 1)] for k in range(4)]

    def matrix(dst, a00, a01, a11):
        dst[0:OB, 0:OB] = a00
        dst[0:OB, OB : 2 * OB] = a01
        dst[OB : 2 * OB, OB : 2 * OB] = a11
        dst[OB : 2 * OB, 0:OB] = flip(a01)

    n_orb = 2 * OB
    row_id = lax.broadcasted_iota(jnp.int32, (n_orb, 128), 0)
    lane_id = lax.broadcasted_iota(jnp.int32, (n_orb, 128), 1)
    work[0] = (lane_id == row_id + n_orb).astype(jnp.float32)
    matrix(work.at[0], *sums(0)[:3])

    def eliminate(step, m):
        k = 2 * step
        row0 = jnp.sum(jnp.where(row_id == k, m, 0.0), axis=0, keepdims=True)
        row1 = jnp.sum(jnp.where(row_id == k + 1, m, 0.0), axis=0, keepdims=True)
        col0 = jnp.sum(jnp.where(lane_id == k, m, 0.0), axis=1, keepdims=True)
        col1 = jnp.sum(jnp.where(lane_id == k + 1, m, 0.0), axis=1, keepdims=True)

        def entry(row, at):
            return jnp.sum(jnp.where(lane_id[:1] == at, row, 0.0), axis=1, keepdims=True)

        inv0 = 1.0 / entry(row0, k)
        ratio0 = entry(row1, k) * inv0
        across0 = entry(row0, k + 1)
        row1 = row1 - ratio0 * row0
        pivot1 = entry(row1, k + 1)
        col1 = col1 - (across0 * inv0) * col0
        factor0 = jnp.where(row_id > k, col0 * inv0, 0.0)
        factor1 = jnp.where(row_id > k + 1, col1 * (1.0 / pivot1), 0.0)
        return m - factor0 * row0 - factor1 * row1

    m = lax.fori_loop(0, n_orb // 2, eliminate, work[0])
    diag = jnp.sum(jnp.where(lane_id == row_id, m, 0.0), axis=1, keepdims=True)
    inverse = m * (1.0 / jnp.sqrt(diag))
    work[0] = inverse

    src = lax.broadcasted_iota(jnp.int32, (128, 128), 0)
    dst = lax.broadcasted_iota(jnp.int32, (128, 128), 1)
    same = src // OB == dst // OB
    mine_rows = work[0, pl.ds(pl.multiple_of(band * OB, OB), OB), :]

    def weights(column):
        pick = (src == n_orb + OB * column + lax.rem(dst, OB)).astype(jnp.float32)
        wide = jnp.dot(mine_rows, pick, precision=HIGHEST, preferred_element_type=jnp.float32)
        return jnp.where(same, jnp.concatenate([wide] * 4, axis=0), 0.0)

    coef[0] = weights(band)
    coef[1] = weights(0)

    def turn(x, carry):
        def times(rows, w):
            return lax.dot_general(
                rows,
                w,
                (((1,), (1,)), ((), ())),
                precision=HIGHEST,
                preferred_element_type=jnp.float32,
            )

        img[x] = times(own(x), coef[0]).reshape(NJ, CY, 128)

        @pl.when(band == 1)
        def _():
            img[x] = img[x] + times(theirs(x), coef[1]).reshape(NJ, CY, 128)

        return carry

    stores = []
    for half in range(2):
        lax.fori_loop(half * CX // 2, (half + 1) * CX // 2, turn, 0)
        for j in range(NJ):
            stores.append(
                pltpu.make_async_copy(
                    img.at[parts[half], j],
                    out_ref.at[0, 0, parts[half], :, pl.ds(128 * j, 128)],
                    out_sem.at[half, j],
                )
            )
            stores[-1].start()

    s00, s01, s10, s11 = sums(1)
    matrix(work.at[1], s00 + flip(s00), s01 + flip(s10), s11 + flip(s11))
    pick = (
        lax.broadcasted_iota(jnp.int32, (128, n_orb), 0)
        == n_orb + lax.broadcasted_iota(jnp.int32, (128, n_orb), 1)
    ).astype(jnp.float32)
    inv = jnp.dot(work[0], pick, precision=HIGHEST, preferred_element_type=jnp.float32)
    left = jnp.dot(
        inv, work[1, :, 0:n_orb], precision=HIGHEST, preferred_element_type=jnp.float32
    )
    proj_ref[...] = lax.dot_general(
        left,
        inv,
        (((1,), (1,)), ((), ())),
        precision=HIGHEST,
        preferred_element_type=jnp.float32,
    )
    for copy in stores:
        copy.wait()
    drain(first)
    drain(second)
    drain(third)
    for copy in across:
        copy.wait_send()


def local(orbitals, potential):
    big = (XO * 2 + CX, JO * 2 + NJ, YO * 2 + CY, 128)
    tile = (CX, NJ, CY, 128)
    vmem = pl.BlockSpec(memory_space=pltpu.VMEM)
    hbm = pl.BlockSpec(memory_space=pl.ANY)
    f32 = jnp.float32
    dma = pltpu.SemaphoreType.DMA
    return pl.pallas_call(
        filter_kernel,
        out_shape=(
            jax.ShapeDtypeStruct((1, 1, CX, CY, CZ * OB), f32),
            jax.ShapeDtypeStruct((2 * OB, 2 * OB), f32),
        ),
        in_specs=[hbm, hbm],
        out_specs=(hbm, vmem),
        scratch_shapes=[
            pltpu.VMEM(big, f32),
            pltpu.VMEM(big, f32),
            pltpu.VMEM(big, f32),
            pltpu.VMEM(tile, f32),
            pltpu.VMEM(tile, f32),
            pltpu.VMEM(tile, f32),
            pltpu.VMEM((2, 4, 8, 128), f32),
            pltpu.VMEM((4, 8, 128), f32),
            pltpu.VMEM((4, 8, 128), f32),
            pltpu.VMEM((1, 8, 128), f32),
            pltpu.VMEM((2, 4, 8, 128), f32),
            pltpu.VMEM((22, 8, 128), f32),
            pltpu.VMEM((2, 2 * OB, 128), f32),
            pltpu.VMEM((2, 128, 128), f32),
            pltpu.VMEM((1, CX, CY, CZ), f32),
            dma((NJ + 1,)),
            dma((2, NJ)),
            dma((3, 6)),
            dma((3, 6)),
            dma((2,)),
            dma((2,)),
            dma((27,)),
            dma((27,)),
        ],
        compiler_params=pltpu.CompilerParams(
            collective_id=0, has_side_effects=True, vmem_limit_bytes=60 << 20
        ),
    )(orbitals, potential)


def solution(mesh):
    return jax.shard_map(
        local,
        mesh=mesh,
        in_specs=(P("dom", "band", None, None, None), P("dom", None, None, None)),
        out_specs=(P("dom", "band", None, None, None), P()),
        check_vma=False,
    )
```

```python
import functools

import jax
import jax.numpy as jnp
from jax import lax
from jax.experimental import pallas as pl
from jax.experimental.pallas import tpu as pltpu
from jax.sharding import PartitionSpec as P

COEFFS = (
    -5369.0 / 1800.0,
    12.0 / 7.0,
    -15.0 / 56.0,
    10.0 / 189.0,
    -1.0 / 112.0,
    2.0 / 1925.0,
    -1.0 / 16632.0,
)
SPACING = 0.32
CENTER = 71.0
HALFWIDTH = 69.0
KINETIC = -0.5 / SPACING**2 / HALFWIDTH
A = tuple(KINETIC * c for c in COEFFS)

CX, CY, CZ, OB = 12, 32, 32, 32
PX, PY, PZ = 8, 4, 4
NJ = CZ * OB // 128
CELLS = PX * CX * PY * CY * PZ * CZ
MESH = pl.DeviceIdType.MESH
HIGHEST = lax.Precision.HIGHEST
XO, JO, YO = 6, 2, 8
OWN = (pl.ds(XO, CX), pl.ds(JO, NJ), pl.ds(YO, CY))


def stencil(field, pot, x):
    lane = lax.broadcasted_iota(jnp.int32, (CY, 128), 1)

    def tile(j, dx=0, dy=0):
        return field[XO + x + dx, JO + j, pl.ds(YO + dy, CY), :]

    def partial(j):
        m2, m1, v, p1 = tile(j - 2), tile(j - 1), tile(j), tile(j + 1)
        t1 = A[3] * m1 + A[1] * v + A[5] * p1
        t2 = A[2] * (v + m1) + A[6] * (p1 + m2)
        t3 = A[3] * v + A[1] * m1 + A[5] * m2
        return (
            pltpu.roll(t1, 96, 1),
            pltpu.roll(t2, 64, 1),
            pltpu.roll(t3, 32, 1),
        )

    out = []
    low = partial(0)
    for j in range(NJ):
        high = partial(j + 1)
        acc = jnp.where(lane < 96, low[0], high[0])
        acc = acc + jnp.where(lane < 64, low[1], high[1])
        acc = acc + jnp.where(lane < 32, low[2], high[2])
        low = high
        acc = acc + pot[x, j] * tile(j)
        for k in range(1, 7):
            terms = tile(j, k) + tile(j, -k) + tile(j, 0, k) + tile(j, 0, -k)
            if k == 4:
                terms = terms + (tile(j + 1) + tile(j - 1))
            acc = acc + A[k] * terms
        out.append(acc)
    return out


def backward_stencil(field, pot, x):
    lane = lax.broadcasted_iota(jnp.int32, (CY, 128), 1)

    def tile(j, dx=0, dy=0):
        return field[XO + x + dx, JO + j, pl.ds(YO + dy, CY), :]

    def partial(j):
        m1, m2 = tile(j - 1), tile(j - 2)
        return (
            pltpu.roll(A[3] * m1, 96, 1),
            pltpu.roll(A[2] * m1 + A[6] * m2, 64, 1),
            pltpu.roll(A[1] * m1 + A[5] * m2, 32, 1),
        )

    out = []
    low = partial(0)
    for j in range(NJ):
        high = partial(j + 1)
        acc = jnp.where(lane < 96, low[0], high[0])
        acc = acc + jnp.where(lane < 64, low[1], high[1])
        acc = acc + jnp.where(lane < 32, low[2], high[2])
        low = high
        acc = acc + 0.5 * pot[x, j] * tile(j)
        for k in range(1, 7):
            terms = tile(j, -k) + tile(j, 0, -k)
            if k == 4:
                terms = terms + tile(j - 1)
            acc = acc + A[k] * terms
        out.append(acc)
    return out


def filter_kernel(
    orb_ref,
    pot_hbm,
    out_ref,
    proj_ref,
    e0,
    e1,
    e2,
    img,
    pot,
    other,
    part,
    gathered,
    halved,
    piece,
    summed,
    recv,
    work,
    coef,
    pot_ref,
    load_sem,
    out_sem,
    hs,
    hr,
    bs,
    br,
    rs,
    rr,
):
    dom = lax.axis_index("dom")
    band = lax.axis_index("band")
    tz = lax.rem(dom, PZ)
    ty = lax.rem(dom // PZ, PY)
    tx = dom // (PY * PZ)
    px, py, pz, core = dom // 32, lax.rem(dom // 8, 4), lax.rem(dom // 2, 4), lax.rem(dom, 2)

    loads = [
        pltpu.make_async_copy(
            orb_ref.at[0, 0, :, :, pl.ds(128 * j, 128)],
            e0.at[pl.ds(XO, CX), JO + j, pl.ds(YO, CY)],
            load_sem.at[j],
        )
        for j in range(NJ)
    ]
    loads.append(pltpu.make_async_copy(pot_hbm, pot_ref, load_sem.at[NJ]))
    for copy in loads:
        copy.start()

    def place(x, y, z, c):
        return ((x * 4 + y) * 4 + z) * 2 + c

    faces = (
        (PY * PZ, tx, PX),
        (PZ, ty, PY),
        (1, tz, PZ),
    )
    twin = (place(px, py, pz, 1 - core), band)
    column = [
        (place(px, py, lax.rem(pz + k, 4), core), lax.rem(band + b, 2))
        for k in range(4)
        for b in range(2)
        if k or b
    ]
    plane = [
        (place(lax.rem(px + i, 4), lax.rem(py + k, 4), pz, core), band)
        for i in range(4)
        for k in range(4)
        if i or k
    ]

    barrier = pltpu.get_barrier_semaphore()
    count = jnp.int32(23)
    for peer in [twin] + column + plane:
        pl.semaphore_signal(barrier, inc=1, device_id=peer, device_id_type=MESH)
    for stride, at, n in faces:
        has_low, has_high = at > 0, at < n - 1
        count = count + has_low.astype(jnp.int32) + has_high.astype(jnp.int32)

        @pl.when(has_low)
        def _():
            pl.semaphore_signal(barrier, inc=1, device_id=(dom - stride, band), device_id_type=MESH)

        @pl.when(has_high)
        def _():
            pl.semaphore_signal(barrier, inc=1, device_id=(dom + stride, band), device_id_type=MESH)

    row = lax.broadcasted_iota(jnp.int32, (CZ, CZ * OB), 0)
    col = lax.broadcasted_iota(jnp.int32, (CZ, CZ * OB), 1)
    spread = (row == col // OB).astype(jnp.float32)

    def spread_pot(x, carry):
        scaled = (pot_ref[0, x] - CENTER) * (1.0 / HALFWIDTH) + 3.0 * A[0]
        wide = jnp.dot(scaled, spread, precision=HIGHEST, preferred_element_type=jnp.float32)
        for j in range(NJ):
            pot[x, j] = wide[:, 128 * j : 128 * (j + 1)]
        return carry

    pl.semaphore_wait(barrier, count)

    def sections(dim):
        sizes = ((XO, CX, 6), (JO, NJ, 2), (YO, CY, 6))
        axis = (0, 2, 1)[dim]
        start, extent, depth = sizes[axis]
        picks = []
        for at in (start, start + extent - depth, start - depth, start + extent):
            index = list(OWN)
            index[axis] = pl.ds(at, depth)
            picks.append(tuple(index))
        return picks

    def halo(field, step):
        copies = []
        for dim, (stride, at, n) in enumerate(faces):
            low_rim, high_rim, below, above = sections(dim)
            up = pltpu.make_async_remote_copy(
                field.at[high_rim],
                field.at[below],
                hs.at[step, 2 * dim],
                hr.at[step, 2 * dim],
                device_id=(lax.rem(dom + stride, 128), band),
                device_id_type=MESH,
            )
            down = pltpu.make_async_remote_copy(
                field.at[low_rim],
                field.at[above],
                hs.at[step, 2 * dim + 1],
                hr.at[step, 2 * dim + 1],
                device_id=(lax.rem(dom - stride + 128, 128), band),
                device_id_type=MESH,
            )
            copies.append((up, at < n - 1, at > 0, below))
            copies.append((down, at > 0, at < n - 1, above))
        return [copies[i] for i in (4, 5, 2, 3, 0, 1)]

    def start(copies, field):
        for copy, sends, receives, landing in copies:

            @pl.when(sends)
            def _():
                copy.start()

        for copy, sends, receives, landing in copies:

            @pl.when(jnp.logical_not(receives))
            def _():
                xs, js, ys = landing

                def clear(i, carry):
                    field[xs.start + i, js, ys] = jnp.zeros((js.size, ys.size, 128), jnp.float32)
                    return carry

                lax.fori_loop(0, xs.size, clear, 0)

    def arrive(copies):
        for copy, sends, receives, landing in copies:

            @pl.when(receives)
            def _():
                copy.wait_recv()

    def drain(copies):
        for copy, sends, receives, landing in copies:

            @pl.when(sends)
            def _():
                copy.wait_send()

    for copy in loads:
        copy.wait()
    first = halo(e0, 0)
    start(first, e0)
    lax.fori_loop(0, CX, spread_pot, 0)
    arrive(first)

    def step_one(x, carry):
        for j, value in enumerate(stencil(e0, pot, x)):
            e1[XO + x, JO + j, pl.ds(YO, CY), :] = value
        return carry

    lax.fori_loop(0, CX, step_one, 0)
    second = halo(e1, 1)
    start(second, e1)
    arrive(second)

    def step_two(x, carry):
        for j, value in enumerate(stencil(e1, pot, x)):
            own = e0[XO + x, JO + j, pl.ds(YO, CY), :]
            e2[XO + x, JO + j, pl.ds(YO, CY), :] = 2.0 * value - own
        return carry

    lax.fori_loop(0, CX, step_two, 0)
    third = halo(e2, 2)[0::2]
    start(third, e2)
    partner = (dom, 1 - band)
    parts = (pl.ds(0, CX // 2), pl.ds(CX // 2, CX // 2))
    across = [
        pltpu.make_async_remote_copy(
            e2.at[pl.ds(XO + planes.start, planes.size), OWN[1], OWN[2]],
            other.at[planes],
            bs.at[at],
            br.at[at],
            device_id=partner,
            device_id_type=MESH,
        )
        for at, planes in enumerate(parts)
    ]
    for copy in across:
        copy.start()

    def own(x):
        return e2[XO + x, pl.ds(JO, NJ), pl.ds(YO, CY), :].reshape(NJ * CY, 128)

    def theirs(x):
        return other[x].reshape(NJ * CY, 128)

    def image(x):
        return img[x].reshape(NJ * CY, 128)

    def gram(left, right, begin, end, wide):
        def add(x, acc):
            return acc + lax.dot_general(
                left(x),
                right(x),
                (((0,), (0,)), ((), ())),
                precision=HIGHEST,
                preferred_element_type=jnp.float32,
            )

        return lax.fori_loop(begin, end, add, jnp.zeros((128, wide), jnp.float32))

    def block(acc, at):
        total = acc[:OB, at : at + OB]
        for g in range(1, 4):
            total = total + acc[OB * g : OB * (g + 1), at + OB * g : at + OB * (g + 1)]
        return total

    def both(x):
        return jnp.concatenate([own(x), image(x)], axis=1)

    def swap(copies):
        for copy in copies:
            copy.start()
        for copy in copies:
            copy.wait()

    def message(source, dest, slot, peer):
        return pltpu.make_async_remote_copy(
            source, dest, rs.at[slot], rr.at[slot], device_id=peer, device_id_type=MESH
        )

    def add_up():
        swap([message(part.at[1 - core], gathered, 0, twin)])
        halved[...] = part[core] + gathered[...]
        swap(
            [
                message(halved.at[lax.rem(pz + (k + 1) // 2, 4)], recv.at[k], 1 + k, peer)
                for k, peer in enumerate(column)
            ]
        )
        total = halved[pz]
        for k in range(len(column)):
            total = total + recv[k]
        piece[0] = total
        swap(
            [
                message(piece.at[0], recv.at[7 + k], 8 + k, peer)
                for k, peer in enumerate(plane)
            ]
        )
        for k in range(len(plane)):
            total = total + recv[7 + k]
        summed[core, pz] = total
        swap(
            [
                message(summed.at[core, pz], summed.at[core, pz], 22 + k, column[2 * k - 1])
                for k in range(1, 4)
            ]
        )
        swap([message(summed.at[core], summed.at[core], 26, twin)])

    def put(which, column, value):
        for half in range(2):
            for t in range(2):
                at = half * (OB // 2) + 8 * t
                part[half, 2 * which + t, :, OB * column : OB * (column + 1)] = value[at : at + 8]

    part[...] = jnp.zeros_like(part)
    arrive(third)

    def step_three(x, carry):
        for j, value in enumerate(backward_stencil(e2, pot, x)):
            img[x, j] = value
        return carry

    lax.fori_loop(0, CX, step_three, 0)
    mine = gram(own, both, 0, CX, 256)

    @pl.when(band == 0)
    def _():
        put(0, 0, block(mine, 0))
        put(1, 0, block(mine, 128))
        across[0].wait_recv()
        crossed = gram(theirs, image, 0, CX // 2, 128)
        across[1].wait_recv()
        crossed = crossed + gram(theirs, image, CX // 2, CX, 128)
        put(1, 2, block(crossed, 0))

    @pl.when(band == 1)
    def _():
        put(0, 2, block(mine, 0))
        put(1, 3, block(mine, 128))
        across[0].wait_recv()
        crossed = gram(theirs, both, 0, CX // 2, 256)
        across[1].wait_recv()
        crossed = crossed + gram(theirs, both, CX // 2, CX, 256)
        put(0, 1, block(crossed, 0))
        put(1, 1, block(crossed, 128))

    add_up()

    eye = (
        lax.broadcasted_iota(jnp.int32, (OB, OB), 0) == lax.broadcasted_iota(jnp.int32, (OB, OB), 1)
    ).astype(jnp.float32)

    def flip(m):
        return lax.dot_general(
            m,
            eye,
            (((0,), (0,)), ((), ())),
            precision=HIGHEST,
            preferred_element_type=jnp.float32,
        )

    def sums(which):
        pieces = [summed[half, 2 * which + t] for half in range(2) for t in range(2)]
        rows = jnp.concatenate(pieces, axis=0) * (1.0 / CELLS)
        return [rows[:, OB * k : OB * (k + 1)] for k in range(4)]

    def matrix(dst, a00, a01, a11):
        dst[0:OB, 0:OB] = a00
        dst[0:OB, OB : 2 * OB] = a01
        dst[OB : 2 * OB, OB : 2 * OB] = a11
        dst[OB : 2 * OB, 0:OB] = flip(a01)

    n_orb = 2 * OB
    row_id = lax.broadcasted_iota(jnp.int32, (n_orb, 128), 0)
    lane_id = lax.broadcasted_iota(jnp.int32, (n_orb, 128), 1)
    work[0] = (lane_id == row_id + n_orb).astype(jnp.float32)
    matrix(work.at[0], *sums(0)[:3])

    def eliminate(step, m):
        k = 2 * step
        row0 = jnp.sum(jnp.where(row_id == k, m, 0.0), axis=0, keepdims=True)
        row1 = jnp.sum(jnp.where(row_id == k + 1, m, 0.0), axis=0, keepdims=True)
        col0 = jnp.sum(jnp.where(lane_id == k, m, 0.0), axis=1, keepdims=True)
        col1 = jnp.sum(jnp.where(lane_id == k + 1, m, 0.0), axis=1, keepdims=True)

        def entry(row, at):
            return jnp.sum(jnp.where(lane_id[:1] == at, row, 0.0), axis=1, keepdims=True)

        inv0 = 1.0 / entry(row0, k)
        ratio0 = entry(row1, k) * inv0
        across0 = entry(row0, k + 1)
        row1 = row1 - ratio0 * row0
        pivot1 = entry(row1, k + 1)
        col1 = col1 - (across0 * inv0) * col0
        factor0 = jnp.where(row_id > k, col0 * inv0, 0.0)
        factor1 = jnp.where(row_id > k + 1, col1 * (1.0 / pivot1), 0.0)
        return m - factor0 * row0 - factor1 * row1

    m = lax.fori_loop(0, n_orb // 2, eliminate, work[0], unroll=4)
    diag = jnp.sum(jnp.where(lane_id == row_id, m, 0.0), axis=1, keepdims=True)
    inverse = m * (1.0 / jnp.sqrt(diag))
    work[0] = inverse

    src = lax.broadcasted_iota(jnp.int32, (128, 128), 0)
    dst = lax.broadcasted_iota(jnp.int32, (128, 128), 1)
    same = src // OB == dst // OB
    mine_rows = work[0, pl.ds(pl.multiple_of(band * OB, OB), OB), :]

    def weights(column):
        pick = (src == n_orb + OB * column + lax.rem(dst, OB)).astype(jnp.float32)
        wide = jnp.dot(mine_rows, pick, precision=HIGHEST, preferred_element_type=jnp.float32)
        return jnp.where(same, jnp.concatenate([wide] * 4, axis=0), 0.0)

    coef[0] = weights(band)
    coef[1] = weights(0)

    def turn(x, carry):
        def times(rows, w):
            return lax.dot_general(
                rows,
                w,
                (((1,), (1,)), ((), ())),
                precision=HIGHEST,
                preferred_element_type=jnp.float32,
            )

        img[x] = times(own(x), coef[0]).reshape(NJ, CY, 128)

        @pl.when(band == 1)
        def _():
            img[x] = img[x] + times(theirs(x), coef[1]).reshape(NJ, CY, 128)

        return carry

    stores = []
    for half in range(2):
        lax.fori_loop(half * CX // 2, (half + 1) * CX // 2, turn, 0)
        for j in range(NJ):
            stores.append(
                pltpu.make_async_copy(
                    img.at[parts[half], j],
                    out_ref.at[0, 0, parts[half], :, pl.ds(128 * j, 128)],
                    out_sem.at[half, j],
                )
            )
            stores[-1].start()

    s00, s01, s10, s11 = sums(1)
    matrix(work.at[1], s00 + flip(s00), s01 + flip(s10), s11 + flip(s11))
    pick = (
        lax.broadcasted_iota(jnp.int32, (128, n_orb), 0)
        == n_orb + lax.broadcasted_iota(jnp.int32, (128, n_orb), 1)
    ).astype(jnp.float32)
    inv = jnp.dot(work[0], pick, precision=HIGHEST, preferred_element_type=jnp.float32)
    left = jnp.dot(
        inv, work[1, :, 0:n_orb], precision=HIGHEST, preferred_element_type=jnp.float32
    )
    proj_ref[...] = lax.dot_general(
        left,
        inv,
        (((1,), (1,)), ((), ())),
        precision=HIGHEST,
        preferred_element_type=jnp.float32,
    )
    for copy in stores:
        copy.wait()
    drain(first)
    drain(second)
    drain(third)
    for copy in across:
        copy.wait_send()


def local(orbitals, potential):
    big = (XO * 2 + CX, JO * 2 + NJ, YO * 2 + CY, 128)
    tile = (CX, NJ, CY, 128)
    vmem = pl.BlockSpec(memory_space=pltpu.VMEM)
    hbm = pl.BlockSpec(memory_space=pl.ANY)
    f32 = jnp.float32
    dma = pltpu.SemaphoreType.DMA
    return pl.pallas_call(
        filter_kernel,
        out_shape=(
            jax.ShapeDtypeStruct((1, 1, CX, CY, CZ * OB), f32),
            jax.ShapeDtypeStruct((2 * OB, 2 * OB), f32),
        ),
        in_specs=[hbm, hbm],
        out_specs=(hbm, vmem),
        scratch_shapes=[
            pltpu.VMEM(big, f32),
            pltpu.VMEM(big, f32),
            pltpu.VMEM(big, f32),
            pltpu.VMEM(tile, f32),
            pltpu.VMEM(tile, f32),
            pltpu.VMEM(tile, f32),
            pltpu.VMEM((2, 4, 8, 128), f32),
            pltpu.VMEM((4, 8, 128), f32),
            pltpu.VMEM((4, 8, 128), f32),
            pltpu.VMEM((1, 8, 128), f32),
            pltpu.VMEM((2, 4, 8, 128), f32),
            pltpu.VMEM((22, 8, 128), f32),
            pltpu.VMEM((2, 2 * OB, 128), f32),
            pltpu.VMEM((2, 128, 128), f32),
            pltpu.VMEM((1, CX, CY, CZ), f32),
            dma((NJ + 1,)),
            dma((2, NJ)),
            dma((3, 6)),
            dma((3, 6)),
            dma((2,)),
            dma((2,)),
            dma((27,)),
            dma((27,)),
        ],
        compiler_params=pltpu.CompilerParams(
            collective_id=0, has_side_effects=True, vmem_limit_bytes=60 << 20
        ),
    )(orbitals, potential)


def solution(mesh):
    return jax.shard_map(
        local,
        mesh=mesh,
        in_specs=(P("dom", "band", None, None, None), P("dom", None, None, None)),
        out_specs=(P("dom", "band", None, None, None), P()),
        check_vma=False,
    )
```
